512 devices in a mesh: batch: 16 (over z_hi, y, core), proto: 32 (over z_lo, x).
Axes of the slice: x: 4, y: 4, z: 16 (z_hi: 2, z_lo: 8; z = z_hi * 8 + z_lo), core: 2. Of those that a mesh axis runs over, the one named last changes fastest.
Arguments:
- hidden: bfloat16 [6144, 2048], P('batch', 'proto'), may hold values from -6 to 6
- w_last: bfloat16 [2048, 256], P('proto'), may hold values from -0.125 to 0.125
- student_protos: bfloat16 [256, 131072], P(None, 'proto'), may hold values from -6 to 6
- teacher_bneck: bfloat16 [6144, 256], P('batch'), may hold values from -8 to 8
- teacher_protos: bfloat16 [256, 131072], P(None, 'proto'), may hold values from -8 to 8
Outputs:
- proto_grad: float32 [256, 131072], P('batch', 'proto')
- weight_grad: float32 [2048, 256], P('proto')
The draws below stay inside these ranges and needn't reach their ends.
All inputs are finite; a program needn't handle non-finite values.
Results may differ from the reference program's by a relative error of at most 0.0029.
The reference program's roundings to bfloat16 on the way (of `student_rows`, `student_cols`, `teacher_rows`, `teacher_cols`, `logit_grad` and `bottleneck_grad`) count: a program that leaves them out, or rounds other values in their place, can miss the bound.
Values may be sent and summed in bfloat16 or wider, within the bound.
A program may use at most 64 MiB of HBM per device.

```python
import jax
import jax.numpy as jnp
from jax import lax

DIM = 256
HID = 2048
PROTOS = 131072
ITERS = 3
CROPS = 6144


def shared_direction(key):
    return jax.random.normal(jax.random.fold_in(key, 911), (DIM,), jnp.float32)


def draw_teacher_bneck(key, part):
    direction = shared_direction(key)
    key = jax.random.fold_in(key, 3)
    coef_key, noise_key = jax.random.split(key)
    along = jnp.clip(jax.random.normal(coef_key, (CROPS,), jnp.float32), -2.5, 2.5)
    noise = jax.random.normal(noise_key, (CROPS, DIM), jnp.float32)
    values = along[:, None] * direction[None, :] + noise
    return jnp.clip(values, -8.0, 8.0).astype(jnp.bfloat16)


def draw_teacher_protos(key, part):
    direction = shared_direction(key)
    key = jax.random.fold_in(key, 5)
    level_key, sign_key, spread_key, noise_key = jax.random.split(key, 4)
    signs = (2 * jax.random.randint(sign_key, (32,), 0, 2) - 1).astype(jnp.float32)
    levels = signs * jax.random.uniform(level_key, (32,), jnp.float32, 0.4, 1.6)
    spread = 0.6 * jax.random.normal(spread_key, (PROTOS,), jnp.float32)
    noise = jax.random.normal(noise_key, (DIM, PROTOS), jnp.float32)
    along = jnp.repeat(levels, PROTOS // 32) + spread
    values = direction[:, None] * along[None, :] + noise
    return jnp.clip(values, -8.0, 8.0).astype(jnp.bfloat16)


def steps_of(key, extent, cuts, smallest, top_value):
    def one(dim, blocks):
        draws = jax.random.uniform(jax.random.fold_in(jax.random.fold_in(key, 6), dim), (blocks,), jnp.float32, smallest / len(cuts), top_value / len(cuts))
        return jnp.repeat(jnp.exp(draws), extent[dim] // blocks).reshape((-1,) + (1,) * (len(extent) - dim - 1))

    gain = one(*cuts[0])
    for cut in cuts[1:]:
        gain = gain * one(*cut)
    return gain


def centred(stream_key, extent, scale, limit, shards=(), kind=jnp.bfloat16):
    values = scale * jax.random.normal(stream_key, extent, jnp.float32)
    if shards:
        values = values * steps_of(stream_key, extent, shards, -0.22, 0.18)
    return jnp.clip(values, -limit, limit).astype(kind)


def setup_inputs(seed: int = 0) -> dict:
    key_of = jax.random.split(jax.random.key(seed), 6)
    hidden = centred(key_of[0], (CROPS, HID), 1.0, 6.0, ((0, 16), (1, 32)))
    w_last = centred(key_of[1], (HID, DIM), HID ** -0.5, 0.125, ((0, 32),))
    student_protos = centred(key_of[2], (DIM, PROTOS), 1.0, 6.0, ((1, 32),))
    teacher_bneck = draw_teacher_bneck(jax.random.fold_in(key_of[5], 71), 0)
    teacher_protos = draw_teacher_protos(jax.random.fold_in(key_of[5], 71), 0)
    return {"hidden": hidden, "w_last": w_last, "student_protos": student_protos, "teacher_bneck": teacher_bneck, "teacher_protos": teacher_protos}


epsilon = 1e-06

def row_unit(values):
    floats = values.astype(jnp.float32)
    return (floats * lax.rsqrt(lax.optimization_barrier(jnp.sum(floats * floats, axis=1)) + epsilon)[:, None]).astype(jnp.bfloat16)

def column_unit(values):
    floats = values.astype(jnp.float32)
    scale = lax.rsqrt(lax.optimization_barrier(jnp.sum(floats * floats, axis=0)) + epsilon)
    return (scale, floats * scale[None, :])

def reference(hidden, w_last, student_protos, teacher_bneck, teacher_protos):
    block_width = min(8192, PROTOS)
    block_count = PROTOS // block_width
    bottleneck = jnp.dot(hidden, w_last, preferred_element_type=jnp.float32)
    row_scale = lax.rsqrt(lax.optimization_barrier(jnp.sum(bottleneck * bottleneck, axis=1)) + epsilon)
    unit_rows = bottleneck * row_scale[:, None]
    student_rows = unit_rows.astype(jnp.bfloat16)
    col_scale, unit_cols = column_unit(student_protos)
    student_cols = unit_cols.astype(jnp.bfloat16)
    teacher_rows = row_unit(teacher_bneck)
    teacher_scale, teacher_float = column_unit(teacher_protos)
    teacher_cols = teacher_float.astype(jnp.bfloat16)

    def blocks(matrix):
        return matrix.reshape(matrix.shape[0], block_count, block_width).transpose(1, 0, 2)
    teacher_exp = lax.map(lambda piece: jnp.exp(25.0 * jnp.dot(teacher_rows, piece, preferred_element_type=jnp.float32)), blocks(teacher_cols))
    crop_scale = jnp.ones((CROPS,), jnp.float32)
    proto_scale = jnp.ones((block_count, block_width), jnp.float32)
    for sweep in range(ITERS):
        proto_mass = lax.optimization_barrier(jnp.sum(teacher_exp * crop_scale[None, :, None], axis=1))
        proto_scale = 1.0 / (PROTOS * proto_mass)
        crop_mass = lax.optimization_barrier(jnp.sum(teacher_exp * proto_scale[:, None, :], axis=(0, 2)))
        crop_scale = 1.0 / (CROPS * crop_mass)
    student_blocks = blocks(student_cols)
    totals = lax.optimization_barrier(jnp.sum(lax.map(lambda piece: lax.optimization_barrier(jnp.sum(jnp.exp(10.0 * jnp.dot(student_rows, piece, preferred_element_type=jnp.float32)), axis=1)), student_blocks), axis=0))

    def backward(row_grad, pieces):
        exp_block, cols_block, unit_block, scale_block, proto_block = pieces
        probs = jnp.exp(10.0 * jnp.dot(student_rows, cols_block, preferred_element_type=jnp.float32)) / totals[:, None]
        targets = (CROPS * crop_scale)[:, None] * exp_block * proto_block[None, :]
        logit_grad = ((probs - targets) * (PROTOS / 128 * 10.0)).astype(jnp.bfloat16)
        row_grad = row_grad + lax.dot_general(logit_grad, cols_block, (((1,), (1,)), ((), ())), preferred_element_type=jnp.float32)
        col_grad = lax.dot_general(student_rows, logit_grad, (((0,), (0,)), ((), ())), preferred_element_type=jnp.float32)
        column_dot = lax.optimization_barrier(jnp.sum(unit_block * col_grad, axis=0))
        return (row_grad, scale_block[None, :] * (col_grad - unit_block * column_dot[None, :]))
    row_grad, grad_blocks = lax.scan(backward, jnp.zeros((CROPS, DIM), jnp.float32), (teacher_exp, student_blocks, blocks(unit_cols), col_scale.reshape(block_count, block_width), proto_scale))
    proto_grad = grad_blocks.transpose(1, 0, 2).reshape(DIM, PROTOS)
    bottleneck_grad = (row_scale[:, None] * (row_grad - unit_rows * lax.optimization_barrier(jnp.sum(unit_rows * row_grad, axis=1))[:, None])).astype(jnp.bfloat16)
    weight_grad = lax.dot_general(hidden, bottleneck_grad, (((0,), (0,)), ((), ())), preferred_element_type=jnp.float32)
    return (proto_grad, weight_grad)
```

```python
import functools

import jax
import jax.numpy as jnp
from jax import lax
from jax.experimental import pallas as pl
from jax.experimental.pallas import tpu as pltpu
from jax.sharding import PartitionSpec as P

PROTOS = 131072
CROPS = 6144
ITERS = 3
EPS = 1e-06
F32 = jnp.float32
BF16 = jnp.bfloat16
MESH = pl.DeviceIdType.MESH

ROWS = 384
COLS = 4096
DIM = 256
CHUNK = 512
NCHUNK = COLS // CHUNK
LANES = 128
NX, NZ, NY = 4, 8, 4
OWN = 16
SHARDS = 6


def ds(start, size):
    return pl.ds(pl.multiple_of(start, size), size)


def kernel(
    hidden, w_last, sp, tb, tp, out_pg, out_wg,
    kexp, sexp, scols, cscale, trows, ub, wide, vrow, acc, sacc, part,
    xrecv, zsrc, zrecv, unit, rscale, srows, rowg, rxrecv, rzsrc, rzrecv, brows,
    nb, fsrc, fb, pm, pmt, colall, crecv, ysend, yrecv, zhsend, zhrecv, total,
    wsrc, wrecv, wfsrc, wfrecv, wfull,
    nb_s, nb_r, fb_s, fb_r, pm_s, pm_r, x_s, x_r, z_s, z_r, az_s, az_r, ax_s, ax_r,
    c_s, c_r, y_s, y_r, zh_s, zh_r, w_s, w_r, wf_s, wf_r, wg_s, wg_r,
):
    b = lax.axis_index("batch")
    p = lax.axis_index("proto")
    zh = b // 8
    k = b % 8
    y = k // 2
    c = b % 2
    z = p // NX
    x = p % NX

    def near(d):
        return {"batch": zh * 8 + (k + d) % 8, "proto": p}

    def far():
        return {"batch": (1 - zh) * 8 + k, "proto": p}

    def core():
        return {"batch": zh * 8 + y * 2 + (1 - c), "proto": p}

    def along_y(d):
        return {"batch": zh * 8 + ((y + d) % NY) * 2 + c, "proto": p}

    def along_x(d):
        return {"batch": b, "proto": z * NX + (x + d) % NX}

    def at_z(j):
        return {"batch": b, "proto": j * NX + x}

    def group(d):
        return {"batch": b, "proto": (p + d) % 32}

    def remote(src, dst, ss, rs, dev):
        return pltpu.make_async_remote_copy(
            src_ref=src, dst_ref=dst, send_sem=ss, recv_sem=rs, device_id=dev, device_id_type=MESH
        )

    def await_bytes(ref, sem):
        pltpu.make_async_copy(ref, ref, sem).wait()

    barrier = pltpu.get_barrier_semaphore()

    def greet(dev):
        pl.semaphore_signal(barrier, inc=1, device_id=dev, device_id_type=MESH)

    for d in range(1, 8):
        greet(near(d))
    greet(far())
    for d in range(1, 32):
        greet(group(d))

    t = tb[...].astype(F32)
    trows[...] = (t * lax.rsqrt(jnp.sum(t * t, axis=1, keepdims=True) + EPS)).astype(BF16)

    def teacher_chunk(i, _):
        cols = ds(i * CHUNK, CHUNK)
        f = tp[:, cols].astype(F32)
        tc = (f * lax.rsqrt(jnp.sum(f * f, axis=0, keepdims=True) + EPS)).astype(BF16)
        e = jnp.exp(25.0 * jnp.dot(trows[...], tc, preferred_element_type=F32))
        kexp[:, cols] = e
        wide[0:1, cols] = jnp.sum(e, axis=0, keepdims=True)
        return 0

    lax.fori_loop(0, NCHUNK, teacher_chunk, 0)
    part[...] = jnp.dot(hidden[...], w_last[...], preferred_element_type=F32)
    pl.semaphore_wait(barrier, 39)

    def pack(s):
        for j in range(32):
            nb[s, k, j : j + 1, :] = wide[0:1, j * LANES : (j + 1) * LANES]

    def near_send(s):
        for d in range(1, 8):
            remote(nb.at[s, k], nb.at[s, k], nb_s.at[s], nb_r.at[s], near(d)).start()

    def near_wait(s):
        await_bytes(nb.at[s, pl.ds(0, 7)], nb_r.at[s])

    def far_send(s):
        fsrc[s] = jnp.sum(nb[s], axis=0)
        remote(fsrc.at[s], fb.at[s], fb_s.at[s], fb_r.at[s], far()).start()

    def far_wait(s):
        remote(fsrc.at[s], fb.at[s], fb_s.at[s], fb_r.at[s], far()).wait()
        await_bytes(nb.at[s, pl.ds(0, 7)], nb_s.at[s])
        return fsrc[s] + fb[s]

    def unpack(v):
        for j in range(32):
            vrow[0:1, j * LANES : (j + 1) * LANES] = v[j : j + 1, :]

    def lanes_of(ref, i):
        blk = ref[i * LANES : (i + 1) * LANES, :]
        return jnp.sum(blk.T, axis=0, keepdims=True)

    def rows_of(v):
        return jnp.broadcast_to(v, (LANES, LANES)).T

    def group_send(buf, s):
        for d in range(1, 32):
            remote(buf.at[p], buf.at[p], pm_s.at[s], pm_r.at[s], group(d)).start()

    def group_wait(buf, s):
        await_bytes(buf.at[pl.ds(0, 31)], pm_r.at[s])
        await_bytes(buf.at[pl.ds(0, 31)], pm_s.at[s])
        return jnp.sum(buf[...], axis=0)

    def row_pass():
        def block(r, _):
            rows = ds(r * 64, 64)

            def step(i, a):
                q = kexp[rows, ds(i * CHUNK, CHUNK)] * vrow[0:1, ds(i * CHUNK, CHUNK)]
                for j in range(CHUNK // LANES):
                    a = a + q[:, j * LANES : (j + 1) * LANES]
                return a

            acc[rows, :] = lax.fori_loop(0, NCHUNK, step, jnp.zeros((64, LANES), F32))
            return 0

        lax.fori_loop(0, ROWS // 64, block, 0)

    def col_pass():
        def step(i, _):
            for j in range(2):
                cols = ds(i * 256 + j * LANES, LANES)
                wide[0:1, cols] = jnp.sum(kexp[:, cols] * ub[...], axis=0, keepdims=True)
            return 0

        lax.fori_loop(0, COLS // 256, step, 0)

    def rs_x_send(s, src, dst):
        for d in range(1, NX):
            rows = ds(((x + d) % NX) * 96, 96)
            remote(src.at[rows], dst.at[d - 1], x_s.at[s], x_r.at[s], along_x(d)).start()

    def rs_z_send(s, src, xr, zs, zr):
        await_bytes(xr, x_r.at[s])
        red = src[ds(x * 96, 96), :] + xr[0] + xr[1] + xr[2]
        zs[...] = red.reshape(SHARDS, OWN, DIM)
        for j in range(SHARDS):
            @pl.when(z != j + 1)
            def _():
                remote(zs.at[j], zr.at[z], z_s.at[s], z_r.at[s], at_z(j + 1)).start()

    owner = jnp.logical_and(z >= 1, z <= SHARDS)

    def rs_z_wait(s, zs, zr):
        await_bytes(zr.at[pl.ds(0, 7)], z_r.at[s])
        zr[z] = zs[z - 1]
        return jnp.sum(zr[...], axis=0)

    def rs_sent(s, xr, zs):
        await_bytes(xr, x_s.at[s])

        @pl.when(owner)
        def _():
            await_bytes(zs.at[pl.ds(0, SHARDS - 1)], z_s.at[s])

        @pl.when(jnp.logical_not(owner))
        def _():
            await_bytes(zs, z_s.at[s])

    def ag_z_send(s, full):
        ref = full.at[x, ds((z - 1) * OWN, OWN)]
        for d in range(1, NZ):
            remote(ref, ref, az_s.at[s], az_r.at[s], at_z((z + d) % NZ)).start()

    def ag_x_send(s, full):
        @pl.when(owner)
        def _():
            await_bytes(full.at[0, pl.ds(0, (SHARDS - 1) * OWN)], az_r.at[s])

        @pl.when(jnp.logical_not(owner))
        def _():
            await_bytes(full.at[0], az_r.at[s])

        for d in range(1, NX):
            remote(full.at[x], full.at[x], ax_s.at[s], ax_r.at[s], along_x(d)).start()

    def ag_wait(s, full):
        await_bytes(full.at[pl.ds(0, 3)], ax_r.at[s])
        await_bytes(full.at[pl.ds(0, 3)], ax_s.at[s])

        @pl.when(owner)
        def _():
            for d in range(1, NZ):
                await_bytes(full.at[0, pl.ds(0, OWN)], az_s.at[s])

        return full[...].reshape(ROWS, DIM)

    pack(0)
    near_send(0)
    rs_x_send(0, part, xrecv)

    def student_cols(i, _):
        cols = ds(i * CHUNK, CHUNK)
        f = sp[:, cols].astype(F32)
        sc = lax.rsqrt(jnp.sum(f * f, axis=0, keepdims=True) + EPS)
        cscale[0:1, cols] = sc
        scols[:, cols] = (f * sc).astype(BF16)
        return 0

    lax.fori_loop(0, NCHUNK, student_cols, 0)
    near_wait(0)
    far_send(0)
    rs_z_send(0, part, xrecv, zsrc, zrecv)
    unpack(1.0 / (PROTOS * far_wait(0)))
    row_pass()
    for i in range(3):
        pm[0, p, 0:1, i * LANES : (i + 1) * LANES] = lanes_of(acc, i)
    group_send(pm.at[0], 0)

    @pl.when(owner)
    def _():
        bott = rs_z_wait(0, zsrc, zrecv)
        sc = lax.rsqrt(jnp.sum(bott * bott, axis=1, keepdims=True) + EPS)
        u = bott * sc
        unit[...] = u
        rscale[...] = jnp.broadcast_to(sc, (OWN, DIM))
        srows[x, ds((z - 1) * OWN, OWN), :] = u.astype(BF16)
        ag_z_send(0, srows)

    def crop_scale(total_):
        return 1.0 / (CROPS * total_)

    def set_u(v):
        for i in range(3):
            ub[i * LANES : (i + 1) * LANES, :] = rows_of(v[:, i * LANES : (i + 1) * LANES])

    set_u(crop_scale(group_wait(pm.at[0], 0)))

    col_pass()
    pack(1)
    near_send(1)
    ag_x_send(0, srows)
    near_wait(1)
    far_send(1)
    sr = ag_wait(0, srows)
    sacc[...] = jnp.zeros_like(sacc)

    def student_chunk(i, _):
        cols = ds(i * CHUNK, CHUNK)
        rows = srows[...].reshape(ROWS, DIM)
        e = jnp.exp(10.0 * jnp.dot(rows, scols[:, cols], preferred_element_type=F32))
        sexp[:, cols] = e
        a = sacc[...]
        for j in range(CHUNK // LANES):
            a = a + e[:, j * LANES : (j + 1) * LANES]
        sacc[...] = a
        return 0

    lax.fori_loop(0, NCHUNK, student_chunk, 0)
    unpack(1.0 / (PROTOS * far_wait(1)))
    row_pass()
    for i in range(3):
        pmt[p, 0:1, i * LANES : (i + 1) * LANES] = lanes_of(acc, i)
        pmt[p, 0:1, ROWS + i * LANES : ROWS + (i + 1) * LANES] = lanes_of(sacc, i)
    group_send(pmt, 1)
    rs_sent(0, xrecv, zsrc)
    both = group_wait(pmt, 1)
    set_u(crop_scale(both[:, :ROWS]))
    gain = PROTOS / 128 * 10.0
    student_scale = gain / both[:, ROWS:]

    col_pass()
    pack(2)
    near_send(2)
    for i in range(3):
        sacc[i * LANES : (i + 1) * LANES, :] = rows_of(student_scale[:, i * LANES : (i + 1) * LANES])
    near_wait(2)
    far_send(2)
    unpack(1.0 / (PROTOS * far_wait(2)))
    row_pass()
    for i in range(3):
        pm[1, p, 0:1, i * LANES : (i + 1) * LANES] = lanes_of(acc, i)
    group_send(pm.at[1], 2)
    rowg[...] = jnp.zeros_like(rowg)
    set_u((gain * CROPS) * crop_scale(group_wait(pm.at[1], 2)))

    def c_copy(i):
        cols = ds(i * CHUNK, CHUNK)
        return remote(
            colall.at[:, 1 - c, :, cols], crecv.at[:, :, cols], c_s.at[i], c_r.at[i], core()
        )

    def y_copy(i, d):
        cols = ds(i * CHUNK, CHUNK)
        return remote(
            ysend.at[(y + d) % NY, :, :, cols], yrecv.at[d - 1, :, :, cols],
            y_s.at[i, d - 1], y_r.at[i, d - 1], along_y(d),
        )

    def zh_copy(i):
        cols = ds(i * CHUNK, CHUNK)
        return remote(zhsend.at[:, cols], zhrecv.at[:, cols], zh_s.at[i], zh_r.at[i], far())

    def y_send(i):
        cols = ds(i * CHUNK, CHUNK)
        c_copy(i).wait()
        for g in range(NY):
            for h in range(2):
                s = colall[h * NY + g, c, :, cols] + crecv[h * NY + g, :, cols]
                crecv[h * NY + g, :, cols] = s
                ysend[g, h, :, cols] = s.astype(BF16)
        for d in range(1, NY):
            y_copy(i, d).start()

    def zh_send(i, _):
        cols = ds(i * CHUNK, CHUNK)
        for d in range(1, NY):
            y_copy(i, d).wait()

        def over_y(h):
            s = crecv[h * NY + y, :, cols]
            for d in range(1, NY):
                s = s + yrecv[d - 1, h, :, cols].astype(F32)
            return s

        total[:, cols] = over_y(zh)
        zhsend[:, cols] = over_y(1 - zh).astype(BF16)
        zh_copy(i).start()
        return 0

    def grad_chunk(i, _):
        cols = ds(i * CHUNK, CHUNK)
        v = vrow[0:1, cols]
        pieces = []
        for j in range(CHUNK // LANES):
            lane = ds(i * CHUNK + j * LANES, LANES)
            vj = v[:, j * LANES : (j + 1) * LANES]
            pieces.append(
                (sexp[:, lane] * sacc[...] - (kexp[:, lane] * vj) * ub[...]).astype(BF16)
            )
        lg = jnp.concatenate(pieces, axis=1)
        rows = srows[...].reshape(ROWS, DIM)
        colg = lax.dot_general(rows, lg, (((0,), (0,)), ((), ())), preferred_element_type=F32)
        colall[:, :, :, cols] = colg.reshape(8, 2, OWN, CHUNK)
        c_copy(i).start()
        rowg[...] += lax.dot_general(
            lg, scols[:, cols], (((1,), (1,)), ((), ())), preferred_element_type=F32
        )
        un = sp[:, cols].astype(F32) * cscale[0:1, cols]
        wide[0:1, cols] = jnp.sum(un * colg, axis=0, keepdims=True)

        @pl.when(i > 0)
        def _():
            y_send(i - 1)

        return 0

    lax.fori_loop(0, NCHUNK, grad_chunk, 0)
    rs_x_send(1, rowg, rxrecv)
    pack(3)
    near_send(3)
    y_send(NCHUNK - 1)
    rs_z_send(1, rowg, rxrecv, rzsrc, rzrecv)
    near_wait(3)
    far_send(3)
    lax.fori_loop(0, 4, zh_send, 0)

    @pl.when(owner)
    def _():
        g = rs_z_wait(1, rzsrc, rzrecv)
        u = unit[...]
        dot = jnp.sum(u * g, axis=1, keepdims=True)
        brows[x, ds((z - 1) * OWN, OWN), :] = (rscale[...] * (g - u * dot)).astype(BF16)
        ag_z_send(1, brows)

    lax.fori_loop(4, NCHUNK, zh_send, 0)
    ag_x_send(1, brows)
    unpack(far_wait(3))
    bg = ag_wait(1, brows)
    wg = lax.dot_general(hidden[...], bg, (((0,), (0,)), ((), ())), preferred_element_type=F32)
    wsrc[...] = wg.reshape(8, 8, DIM)
    for d in range(1, 8):
        remote(wsrc.at[(k + d) % 8], wrecv.at[k], w_s, w_r, near(d)).start()

    def finish(i, _):
        cols = ds(i * CHUNK, CHUNK)
        zh_copy(i).wait()
        s = total[:, cols] + zhrecv[:, cols].astype(F32)
        sc = cscale[0:1, cols]
        un = sp[ds(b * OWN, OWN), cols].astype(F32) * sc
        out_pg[:, cols] = sc * (s - un * vrow[0:1, cols])
        return 0

    await_bytes(wrecv.at[pl.ds(0, 7)], w_r)
    wrecv[k] = wsrc[k]
    wfsrc[...] = jnp.sum(wrecv[...], axis=0)
    wf = remote(wfsrc, wfrecv, wf_s, wf_r, far())
    wf.start()
    lax.fori_loop(0, NCHUNK, finish, 0)
    rs_sent(1, rxrecv, rzsrc)
    await_bytes(wsrc.at[pl.ds(0, 7)], w_s)
    wf.wait()
    wfull[k] = wfsrc[...] + wfrecv[...]
    for d in range(1, 8):
        remote(wfull.at[k], wfull.at[k], wg_s, wg_r, near(d)).start()
    await_bytes(wfull.at[pl.ds(0, 7)], wg_r)
    await_bytes(wfull.at[pl.ds(0, 7)], wg_s)
    out_wg[...] = wfull[...].reshape(64, DIM)


def per_device(hidden, w_last, student_protos, teacher_bneck, teacher_protos):
    vm = pltpu.VMEM
    dma = pltpu.SemaphoreType.DMA
    scratch = [
        vm((ROWS, COLS), F32), vm((ROWS, COLS), F32), vm((DIM, COLS), BF16), vm((8, COLS), F32),
        vm((ROWS, DIM), BF16), vm((ROWS, LANES), F32), vm((8, COLS), F32), vm((8, COLS), F32),
        vm((ROWS, LANES), F32), vm((ROWS, LANES), F32), vm((ROWS, DIM), F32),
        vm((3, 96, DIM), F32), vm((SHARDS, OWN, DIM), F32), vm((NZ, OWN, DIM), F32),
        vm((OWN, DIM), F32), vm((OWN, DIM), F32), vm((NX, 96, DIM), BF16), vm((ROWS, DIM), F32),
        vm((3, 96, DIM), F32), vm((SHARDS, OWN, DIM), F32), vm((NZ, OWN, DIM), F32),
        vm((NX, 96, DIM), BF16),
        vm((4, 8, 32, LANES), F32), vm((4, 32, LANES), F32), vm((4, 32, LANES), F32),
        vm((2, 32, 1, ROWS), F32), vm((32, 1, 2 * ROWS), F32),
        vm((8, 2, OWN, COLS), F32), vm((8, OWN, COLS), F32), vm((NY, 2, OWN, COLS), BF16),
        vm((3, 2, OWN, COLS), BF16), vm((OWN, COLS), BF16), vm((OWN, COLS), BF16),
        vm((OWN, COLS), F32),
        vm((8, 8, DIM), F32), vm((8, 8, DIM), F32), vm((8, DIM), F32), vm((8, DIM), F32),
        vm((8, 8, DIM), F32),
        dma((4,)), dma((4,)), dma((4,)), dma((4,)), dma((3,)), dma((3,)),
        dma((2,)), dma((2,)), dma((2,)), dma((2,)), dma((2,)), dma((2,)), dma((2,)), dma((2,)),
        dma((NCHUNK,)), dma((NCHUNK,)), dma((NCHUNK, 3)), dma((NCHUNK, 3)),
        dma((NCHUNK,)), dma((NCHUNK,)), dma, dma, dma, dma, dma, dma,
    ]
    spec = pl.BlockSpec(memory_space=pltpu.VMEM)
    return pl.pallas_call(
        kernel,
        out_shape=(
            jax.ShapeDtypeStruct((OWN, COLS), F32),
            jax.ShapeDtypeStruct((64, DIM), F32),
        ),
        in_specs=[spec] * 5,
        out_specs=(spec, spec),
        scratch_shapes=scratch,
        compiler_params=pltpu.CompilerParams(
            collective_id=0, has_side_effects=True, vmem_limit_bytes=60 * 1024 * 1024
        ),
        name="dino_head",
    )(hidden, w_last, student_protos, teacher_bneck, teacher_protos)


def solution(mesh):
    placed = (
        P("batch", "proto"),
        P("proto", None),
        P(None, "proto"),
        P("batch", None),
        P(None, "proto"),
    )
    return jax.shard_map(
        per_device,
        mesh=mesh,
        in_specs=placed,
        out_specs=(P("batch", "proto"), P("proto", None)),
        check_vma=False,
    )
```

```python
import functools

import jax
import jax.numpy as jnp
from jax import lax
from jax.experimental import pallas as pl
from jax.experimental.pallas import tpu as pltpu
from jax.sharding import PartitionSpec as P

PROTOS = 131072
CROPS = 6144
ITERS = 3
EPS = 1e-06
F32 = jnp.float32
BF16 = jnp.bfloat16
MESH = pl.DeviceIdType.MESH

ROWS = 384
COLS = 4096
DIM = 256
CHUNK = 512
NCHUNK = COLS // CHUNK
LANES = 128
NX, NZ, NY = 4, 8, 4
ZH0, ZH1 = 0, 4
OWN = 16
SHARDS = 6


def ds(start, size):
    return pl.ds(pl.multiple_of(start, size), size)


def kernel(
    hidden, w_last, sp, tb, tp, out_pg, out_wg,
    kexp, sexp, scols, cscale, trows, ub, wide, vrow, acc, sacc, part,
    xrecv, zsrc, zrecv, unit, rscale, srows, rowg, rxrecv, rzsrc, rzrecv, brows,
    nb, fsrc, fb, pm, pmt, lgs, colall, crecv, ysend, yrecv, zhsend, zhrecv, total,
    wsrc, wrecv, wfsrc, wfrecv, wfull,
    nb_s, nb_r, fb_s, fb_r, pm_s, pm_r, x_s, x_r, z_s, z_r, az_s, az_r, ax_s, ax_r,
    c_s, c_r, y_s, y_r, zh_s, zh_r, w_s, w_r, wf_s, wf_r, wg_s, wg_r,
):
    b = lax.axis_index("batch")
    p = lax.axis_index("proto")
    zh = b // 8
    k = b % 8
    y = k // 2
    c = b % 2
    z = p // NX
    x = p % NX

    def near(d):
        return {"batch": zh * 8 + (k + d) % 8, "proto": p}

    def far():
        return {"batch": (1 - zh) * 8 + k, "proto": p}

    def core():
        return {"batch": zh * 8 + y * 2 + (1 - c), "proto": p}

    def along_y(d):
        return {"batch": zh * 8 + ((y + d) % NY) * 2 + c, "proto": p}

    def along_x(d):
        return {"batch": b, "proto": z * NX + (x + d) % NX}

    def at_z(j):
        return {"batch": b, "proto": j * NX + x}

    def group(d):
        return {"batch": b, "proto": (p + d) % 32}

    def remote(src, dst, ss, rs, dev):
        return pltpu.make_async_remote_copy(
            src_ref=src, dst_ref=dst, send_sem=ss, recv_sem=rs, device_id=dev, device_id_type=MESH
        )

    def await_bytes(ref, sem):
        pltpu.make_async_copy(ref, ref, sem).wait()

    barrier = pltpu.get_barrier_semaphore()

    def greet(dev):
        pl.semaphore_signal(barrier, inc=1, device_id=dev, device_id_type=MESH)

    for d in range(1, 8):
        greet(near(d))
    greet(far())
    for d in range(1, 32):
        greet(group(d))

    t = tb[...].astype(F32)
    trows[...] = (t * lax.rsqrt(jnp.sum(t * t, axis=1, keepdims=True) + EPS)).astype(BF16)

    def teacher_chunk(i, _):
        cols = ds(i * CHUNK, CHUNK)
        f = tp[:, cols].astype(F32)
        tc = (f * lax.rsqrt(jnp.sum(f * f, axis=0, keepdims=True) + EPS)).astype(BF16)
        e = jnp.exp(25.0 * jnp.dot(trows[...], tc, preferred_element_type=F32))
        kexp[:, cols] = e
        wide[0:1, cols] = jnp.sum(e, axis=0, keepdims=True)
        return 0

    lax.fori_loop(0, NCHUNK, teacher_chunk, 0)
    part[...] = jnp.dot(hidden[...], w_last[...], preferred_element_type=F32)
    pl.semaphore_wait(barrier, 39)

    def pack(s):
        for j in range(32):
            nb[s, k, j : j + 1, :] = wide[0:1, j * LANES : (j + 1) * LANES]

    def near_send(s):
        for d in range(1, 8):
            remote(nb.at[s, k], nb.at[s, k], nb_s.at[s], nb_r.at[s], near(d)).start()

    def near_wait(s):
        await_bytes(nb.at[s, pl.ds(0, 7)], nb_r.at[s])

    def far_send(s):
        fsrc[s] = jnp.sum(nb[s], axis=0)
        remote(fsrc.at[s], fb.at[s], fb_s.at[s], fb_r.at[s], far()).start()

    def far_wait(s):
        remote(fsrc.at[s], fb.at[s], fb_s.at[s], fb_r.at[s], far()).wait()
        await_bytes(nb.at[s, pl.ds(0, 7)], nb_s.at[s])
        return fsrc[s] + fb[s]

    def unpack(v):
        for j in range(32):
            vrow[0:1, j * LANES : (j + 1) * LANES] = v[j : j + 1, :]

    def lanes_of(ref, i):
        blk = ref[i * LANES : (i + 1) * LANES, :]
        return jnp.sum(blk.T, axis=0, keepdims=True)

    def rows_of(v):
        return jnp.broadcast_to(v, (LANES, LANES)).T

    def group_send(buf, s):
        for d in range(1, 32):
            remote(buf.at[p], buf.at[p], pm_s.at[s], pm_r.at[s], group(d)).start()

    def group_wait(buf, s):
        await_bytes(buf.at[pl.ds(0, 31)], pm_r.at[s])
        await_bytes(buf.at[pl.ds(0, 31)], pm_s.at[s])
        return jnp.sum(buf[...], axis=0)

    def row_pass():
        def block(r, _):
            rows = ds(r * 64, 64)

            def step(i, a):
                q = kexp[rows, ds(i * CHUNK, CHUNK)] * vrow[0:1, ds(i * CHUNK, CHUNK)]
                for j in range(CHUNK // LANES):
                    a = a + q[:, j * LANES : (j + 1) * LANES]
                return a

            acc[rows, :] = lax.fori_loop(0, NCHUNK, step, jnp.zeros((64, LANES), F32))
            return 0

        lax.fori_loop(0, ROWS // 64, block, 0)

    def col_pass():
        def step(i, _):
            for j in range(2):
                cols = ds(i * 256 + j * LANES, LANES)
                wide[0:1, cols] = jnp.sum(kexp[:, cols] * ub[...], axis=0, keepdims=True)
            return 0

        lax.fori_loop(0, COLS // 256, step, 0)

    def rs_x_send(s, src, dst):
        for d in range(1, NX):
            rows = ds(((x + d) % NX) * 96, 96)
            remote(src.at[rows], dst.at[d - 1], x_s.at[s], x_r.at[s], along_x(d)).start()

    def rs_z_send(s, src, xr, zs, zr):
        await_bytes(xr, x_r.at[s])
        red = src[ds(x * 96, 96), :] + xr[0] + xr[1] + xr[2]
        zs[...] = red.reshape(SHARDS, OWN, DIM)
        for j in range(SHARDS):
            @pl.when(z != j + 1)
            def _():
                remote(zs.at[j], zr.at[z], z_s.at[s], z_r.at[s], at_z(j + 1)).start()

    owner = jnp.logical_and(z >= 1, z <= SHARDS)

    def rs_z_wait(s, zs, zr):
        await_bytes(zr.at[pl.ds(0, 7)], z_r.at[s])
        zr[z] = zs[z - 1]
        return jnp.sum(zr[...], axis=0)

    def rs_sent(s, xr, zs):
        await_bytes(xr, x_s.at[s])

        @pl.when(owner)
        def _():
            await_bytes(zs.at[pl.ds(0, SHARDS - 1)], z_s.at[s])

        @pl.when(jnp.logical_not(owner))
        def _():
            await_bytes(zs, z_s.at[s])

    def ag_z_send(s, full):
        ref = full.at[x, ds((z - 1) * OWN, OWN)]
        for d in range(1, NZ):
            remote(ref, ref, az_s.at[s], az_r.at[s], at_z((z + d) % NZ)).start()

    def ag_x_send(s, full):
        @pl.when(owner)
        def _():
            await_bytes(full.at[0, pl.ds(0, (SHARDS - 1) * OWN)], az_r.at[s])

        @pl.when(jnp.logical_not(owner))
        def _():
            await_bytes(full.at[0], az_r.at[s])

        for d in range(1, NX):
            remote(full.at[x], full.at[x], ax_s.at[s], ax_r.at[s], along_x(d)).start()

    def ag_wait(s, full):
        await_bytes(full.at[pl.ds(0, 3)], ax_r.at[s])
        await_bytes(full.at[pl.ds(0, 3)], ax_s.at[s])

        @pl.when(owner)
        def _():
            for d in range(1, NZ):
                await_bytes(full.at[0, pl.ds(0, OWN)], az_s.at[s])

        return full[...].reshape(ROWS, DIM)

    pack(0)
    near_send(0)
    rs_x_send(0, part, xrecv)

    def student_cols(i, _):
        cols = ds(i * CHUNK, CHUNK)
        f = sp[:, cols].astype(F32)
        sc = lax.rsqrt(jnp.sum(f * f, axis=0, keepdims=True) + EPS)
        cscale[0:1, cols] = sc
        scols[:, cols] = (f * sc).astype(BF16)
        return 0

    lax.fori_loop(0, NCHUNK, student_cols, 0)
    near_wait(0)
    far_send(0)
    rs_z_send(0, part, xrecv, zsrc, zrecv)
    unpack(1.0 / (PROTOS * far_wait(0)))
    row_pass()
    for i in range(3):
        pm[0, p, 0:1, i * LANES : (i + 1) * LANES] = lanes_of(acc, i)
    group_send(pm.at[0], 0)

    @pl.when(owner)
    def _():
        bott = rs_z_wait(0, zsrc, zrecv)
        sc = lax.rsqrt(jnp.sum(bott * bott, axis=1, keepdims=True) + EPS)
        u = bott * sc
        unit[...] = u
        rscale[...] = jnp.broadcast_to(sc, (OWN, DIM))
        srows[x, ds((z - 1) * OWN, OWN), :] = u.astype(BF16)
        ag_z_send(0, srows)

    def crop_scale(total_):
        return 1.0 / (CROPS * total_)

    def set_u(v):
        for i in range(3):
            ub[i * LANES : (i + 1) * LANES, :] = rows_of(v[:, i * LANES : (i + 1) * LANES])

    set_u(crop_scale(group_wait(pm.at[0], 0)))

    col_pass()
    pack(1)
    near_send(1)
    ag_x_send(0, srows)
    near_wait(1)
    far_send(1)
    sr = ag_wait(0, srows)
    sacc[...] = jnp.zeros_like(sacc)

    def student_chunk(i, _):
        cols = ds(i * CHUNK, CHUNK)
        rows = srows[...].reshape(ROWS, DIM)
        e = jnp.exp(10.0 * jnp.dot(rows, scols[:, cols], preferred_element_type=F32))
        sexp[:, cols] = e
        a = sacc[...]
        for j in range(CHUNK // LANES):
            a = a + e[:, j * LANES : (j + 1) * LANES]
        sacc[...] = a
        return 0

    lax.fori_loop(0, NCHUNK, student_chunk, 0)
    unpack(1.0 / (PROTOS * far_wait(1)))
    row_pass()
    for i in range(3):
        pmt[p, 0:1, i * LANES : (i + 1) * LANES] = lanes_of(acc, i)
        pmt[p, 0:1, ROWS + i * LANES : ROWS + (i + 1) * LANES] = lanes_of(sacc, i)
    group_send(pmt, 1)
    rs_sent(0, xrecv, zsrc)
    both = group_wait(pmt, 1)
    set_u(crop_scale(both[:, :ROWS]))
    gain = PROTOS / 128 * 10.0
    student_scale = gain / both[:, ROWS:]

    col_pass()
    pack(2)
    near_send(2)
    for i in range(3):
        sacc[i * LANES : (i + 1) * LANES, :] = rows_of(student_scale[:, i * LANES : (i + 1) * LANES])
    near_wait(2)
    far_send(2)
    unpack(1.0 / (PROTOS * far_wait(2)))
    row_pass()
    for i in range(3):
        pm[1, p, 0:1, i * LANES : (i + 1) * LANES] = lanes_of(acc, i)
    group_send(pm.at[1], 2)
    rowg[...] = jnp.zeros_like(rowg)
    set_u((gain * CROPS) * crop_scale(group_wait(pm.at[1], 2)))

    def c_copy(i):
        cols = ds(i * CHUNK, CHUNK)
        return remote(
            colall.at[:, 1 - c, :, cols], crecv.at[:, :, cols], c_s.at[i], c_r.at[i], core()
        )

    def y_copy(i, d):
        cols = ds(i * CHUNK, CHUNK)
        return remote(
            ysend.at[(y + d) % NY, :, :, cols], yrecv.at[d - 1, :, :, cols],
            y_s.at[i, d - 1], y_r.at[i, d - 1], along_y(d),
        )

    def zh_copy(i):
        cols = ds(i * CHUNK, CHUNK)
        return remote(zhsend.at[:, cols], zhrecv.at[:, cols], zh_s.at[i], zh_r.at[i], far())

    def y_send(i):
        cols = ds(i * CHUNK, CHUNK)
        c_copy(i).wait()
        for g in range(NY):
            for h in range(2):
                s = colall[h * NY + g, c, :, cols] + crecv[h * NY + g, :, cols]
                crecv[h * NY + g, :, cols] = s
                ysend[g, h, :, cols] = s.astype(BF16)
        for d in range(1, NY):
            y_copy(i, d).start()

    def zh_send(i, _):
        cols = ds(i * CHUNK, CHUNK)
        for d in range(1, NY):
            y_copy(i, d).wait()

        def over_y(h):
            s = crecv[h * NY + y, :, cols]
            for d in range(1, NY):
                s = s + yrecv[d - 1, h, :, cols].astype(F32)
            return s

        total[:, cols] = over_y(zh)
        zhsend[:, cols] = over_y(1 - zh).astype(BF16)
        zh_copy(i).start()
        return 0

    def grad_chunk(i, _):
        cols = ds(i * CHUNK, CHUNK)
        v = vrow[0:1, cols]
        pieces = []
        for j in range(CHUNK // LANES):
            lane = ds(i * CHUNK + j * LANES, LANES)
            vj = v[:, j * LANES : (j + 1) * LANES]
            pieces.append(
                (sexp[:, lane] * sacc[...] - (kexp[:, lane] * vj) * ub[...]).astype(BF16)
            )
        lg = jnp.concatenate(pieces, axis=1)
        lgs[:, cols] = lg
        rowg[...] += lax.dot_general(
            lg, scols[:, cols], (((1,), (1,)), ((), ())), preferred_element_type=F32
        )
        return 0

    def column_chunk(i, _):
        cols = ds(i * CHUNK, CHUNK)
        rows = srows[...].reshape(ROWS, DIM)
        colg = lax.dot_general(
            rows, lgs[:, cols], (((0,), (0,)), ((), ())), preferred_element_type=F32
        )
        colall[:, :, :, cols] = colg.reshape(8, 2, OWN, CHUNK)
        c_copy(i).start()
        un = sp[:, cols].astype(F32) * cscale[0:1, cols]
        wide[0:1, cols] = jnp.sum(un * colg, axis=0, keepdims=True)
        return 0

    def y_sends(i, _):
        y_send(i)
        return 0

    lax.fori_loop(0, NCHUNK, grad_chunk, 0)
    rs_x_send(1, rowg, rxrecv)
    lax.fori_loop(0, NCHUNK, column_chunk, 0)
    pack(3)
    near_send(3)
    rs_z_send(1, rowg, rxrecv, rzsrc, rzrecv)
    lax.fori_loop(0, NCHUNK, y_sends, 0)
    near_wait(3)
    far_send(3)
    lax.fori_loop(0, ZH0, zh_send, 0)

    @pl.when(owner)
    def _():
        g = rs_z_wait(1, rzsrc, rzrecv)
        u = unit[...]
        dot = jnp.sum(u * g, axis=1, keepdims=True)
        brows[x, ds((z - 1) * OWN, OWN), :] = (rscale[...] * (g - u * dot)).astype(BF16)
        ag_z_send(1, brows)

    lax.fori_loop(ZH0, ZH1, zh_send, 0)
    ag_x_send(1, brows)
    lax.fori_loop(ZH1, NCHUNK, zh_send, 0)
    unpack(far_wait(3))
    bg = ag_wait(1, brows)
    wg = lax.dot_general(hidden[...], bg, (((0,), (0,)), ((), ())), preferred_element_type=F32)
    wsrc[...] = wg.reshape(8, 8, DIM)
    for d in range(1, 8):
        remote(wsrc.at[(k + d) % 8], wrecv.at[k], w_s, w_r, near(d)).start()

    def finish(i, _):
        cols = ds(i * CHUNK, CHUNK)
        zh_copy(i).wait()
        s = total[:, cols] + zhrecv[:, cols].astype(F32)
        sc = cscale[0:1, cols]
        un = sp[ds(b * OWN, OWN), cols].astype(F32) * sc
        out_pg[:, cols] = sc * (s - un * vrow[0:1, cols])
        return 0

    await_bytes(wrecv.at[pl.ds(0, 7)], w_r)
    wrecv[k] = wsrc[k]
    wfsrc[...] = jnp.sum(wrecv[...], axis=0)
    wf = remote(wfsrc, wfrecv, wf_s, wf_r, far())
    wf.start()
    lax.fori_loop(0, NCHUNK, finish, 0)
    rs_sent(1, rxrecv, rzsrc)
    await_bytes(wsrc.at[pl.ds(0, 7)], w_s)
    wf.wait()
    wfull[k] = wfsrc[...] + wfrecv[...]
    for d in range(1, 8):
        remote(wfull.at[k], wfull.at[k], wg_s, wg_r, near(d)).start()
    await_bytes(wfull.at[pl.ds(0, 7)], wg_r)
    await_bytes(wfull.at[pl.ds(0, 7)], wg_s)
    out_wg[...] = wfull[...].reshape(64, DIM)


def per_device(hidden, w_last, student_protos, teacher_bneck, teacher_protos):
    vm = pltpu.VMEM
    dma = pltpu.SemaphoreType.DMA
    scratch = [
        vm((ROWS, COLS), F32), vm((ROWS, COLS), F32), vm((DIM, COLS), BF16), vm((8, COLS), F32),
        vm((ROWS, DIM), BF16), vm((ROWS, LANES), F32), vm((8, COLS), F32), vm((8, COLS), F32),
        vm((ROWS, LANES), F32), vm((ROWS, LANES), F32), vm((ROWS, DIM), F32),
        vm((3, 96, DIM), F32), vm((SHARDS, OWN, DIM), F32), vm((NZ, OWN, DIM), F32),
        vm((OWN, DIM), F32), vm((OWN, DIM), F32), vm((NX, 96, DIM), BF16), vm((ROWS, DIM), F32),
        vm((3, 96, DIM), F32), vm((SHARDS, OWN, DIM), F32), vm((NZ, OWN, DIM), F32),
        vm((NX, 96, DIM), BF16),
        vm((4, 8, 32, LANES), F32), vm((4, 32, LANES), F32), vm((4, 32, LANES), F32),
        vm((2, 32, 1, ROWS), F32), vm((32, 1, 2 * ROWS), F32),
        vm((ROWS, COLS), BF16), vm((8, 2, OWN, COLS), F32), vm((8, OWN, COLS), F32), vm((NY, 2, OWN, COLS), BF16),
        vm((3, 2, OWN, COLS), BF16), vm((OWN, COLS), BF16), vm((OWN, COLS), BF16),
        vm((OWN, COLS), F32),
        vm((8, 8, DIM), F32), vm((8, 8, DIM), F32), vm((8, DIM), F32), vm((8, DIM), F32),
        vm((8, 8, DIM), F32),
        dma((4,)), dma((4,)), dma((4,)), dma((4,)), dma((3,)), dma((3,)),
        dma((2,)), dma((2,)), dma((2,)), dma((2,)), dma((2,)), dma((2,)), dma((2,)), dma((2,)),
        dma((NCHUNK,)), dma((NCHUNK,)), dma((NCHUNK, 3)), dma((NCHUNK, 3)),
        dma((NCHUNK,)), dma((NCHUNK,)), dma, dma, dma, dma, dma, dma,
    ]
    spec = pl.BlockSpec(memory_space=pltpu.VMEM)
    return pl.pallas_call(
        kernel,
        out_shape=(
            jax.ShapeDtypeStruct((OWN, COLS), F32),
            jax.ShapeDtypeStruct((64, DIM), F32),
        ),
        in_specs=[spec] * 5,
        out_specs=(spec, spec),
        scratch_shapes=scratch,
        compiler_params=pltpu.CompilerParams(
            collective_id=0, has_side_effects=True, vmem_limit_bytes=60 * 1024 * 1024
        ),
        name="dino_head",
    )(hidden, w_last, student_protos, teacher_bneck, teacher_protos)


def solution(mesh):
    placed = (
        P("batch", "proto"),
        P("proto", None),
        P(None, "proto"),
        P("batch", None),
        P(None, "proto"),
    )
    return jax.shard_map(
        per_device,
        mesh=mesh,
        in_specs=placed,
        out_specs=(P("batch", "proto"), P("proto", None)),
        check_vma=False,
    )
```

```python
import functools

import jax
import jax.numpy as jnp
from jax import lax
from jax.experimental import pallas as pl
from jax.experimental.pallas import tpu as pltpu
from jax.sharding import PartitionSpec as P

PROTOS = 131072
CROPS = 6144
ITERS = 3
EPS = 1e-06
F32 = jnp.float32
BF16 = jnp.bfloat16
MESH = pl.DeviceIdType.MESH

ROWS = 384
COLS = 4096
DIM = 256
CHUNK = 512
WIDE = 1024
NCHUNK = COLS // CHUNK
HALF = COLS // 2
LANES = 128
NX, NZ, NY = 4, 8, 4
ZH0, ZH1 = 0, 4
OWN = 16
SHARDS = 6


def ds(start, size):
    return pl.ds(pl.multiple_of(start, size), size)


def kernel(
    hidden_in, w_in, sp_in, tb_in, tp_in, out_pg, out_wg,
    hidden, w_last, sp, tb, tp, in_s, out_s,
    kexp, sexp, scols, cscale, trows, ub, wide, vrow, acc, sacc, part,
    xrecv, zsrc, zrecv, unit, rscale, srows, rowg, rxrecv, rzsrc, rzrecv, brows,
    nb, fsrc, fb, nbh, vh, xb1, zb1, xb, zb, xbs, zbs, kp, tpr, ubp, accp, lgs, colall, crecv, ysend, yrecv, zhsend, zhrecv, total,
    wsrc, wrecv, wfsrc, wfrecv, wfull,
    nb_s, nb_r, fb_s, fb_r, nh_s, nh_r, vh_s, vh_r, xb_s, xb_r, zb_s, zb_r,
    mi_s, mi_r, tx_s, tx_r, x_s, x_r, z_s, z_r, az_s, az_r, ax_s, ax_r,
    c_s, c_r, y_s, y_r, zh_s, zh_r, w_s, w_r, wf_s, wf_r, wg_s, wg_r,
):
    b = lax.axis_index("batch")
    p = lax.axis_index("proto")
    zh = b // 8
    k = b % 8
    y = k // 2
    c = b % 2
    z = p // NX
    x = p % NX

    def near(d):
        return {"batch": zh * 8 + (k + d) % 8, "proto": p}

    def far():
        return {"batch": (1 - zh) * 8 + k, "proto": p}

    def core():
        return {"batch": zh * 8 + y * 2 + (1 - c), "proto": p}

    def along_y(d):
        return {"batch": zh * 8 + ((y + d) % NY) * 2 + c, "proto": p}

    def along_x(d):
        return {"batch": b, "proto": z * NX + (x + d) % NX}

    def at_z(j):
        return {"batch": b, "proto": j * NX + x}

    gz = zh * NZ + z

    def ring(d):
        g = (gz + d) % 16
        return {"batch": (g // NZ) * 8 + k, "proto": (g % NZ) * NX + x}

    def mirror():
        return {"batch": (1 - zh) * 8 + k, "proto": (NZ - 1 - z) * NX + x}

    def remote(src, dst, ss, rs, dev):
        return pltpu.make_async_remote_copy(
            src_ref=src, dst_ref=dst, send_sem=ss, recv_sem=rs, device_id=dev, device_id_type=MESH
        )

    def await_bytes(ref, sem):
        pltpu.make_async_copy(ref, ref, sem).wait()

    def load(src, dst, i):
        return pltpu.make_async_copy(src, dst, in_s.at[i])

    def tp_load(i):
        cols = ds(i * WIDE, WIDE)
        return load(tp_in.at[:, cols], tp.at[:, cols], i)

    loads = [load(tb_in, tb, 4), load(hidden_in, hidden, 5), load(w_in, w_last, 6), load(sp_in, sp, 7)]
    loads[0].start()
    for i in range(COLS // WIDE):
        tp_load(i).start()
    for copy in loads[1:]:
        copy.start()

    barrier = pltpu.get_barrier_semaphore()

    def greet(dev):
        pl.semaphore_signal(barrier, inc=1, device_id=dev, device_id_type=MESH)

    for d in range(1, 8):
        greet(near(d))
    for d in range(1, NX):
        greet(along_x(d))
    for d in range(1, 16):
        greet(ring(d))

    loads[0].wait()
    t = tb[...].astype(F32)
    trows[...] = (t * lax.rsqrt(jnp.sum(t * t, axis=1, keepdims=True) + EPS)).astype(BF16)

    def store_sums(s, i, sums):
        nb[s, k, ds(i * 8, 8), :] = jnp.concatenate(sums, axis=0)

    def teacher_chunk(i, _):
        cols = ds(i * WIDE, WIDE)
        tp_load(i).wait()
        f = tp[:, cols].astype(F32)
        tc = (f * lax.rsqrt(jnp.sum(f * f, axis=0, keepdims=True) + EPS)).astype(BF16)
        e = jnp.exp(25.0 * jnp.dot(trows[...], tc, preferred_element_type=F32))
        tp[:, cols] = tc
        kexp[:, cols] = e
        sums = jnp.sum(e, axis=0, keepdims=True)
        store_sums(0, i, [sums[:, j * LANES : (j + 1) * LANES] for j in range(8)])
        return 0

    lax.fori_loop(0, COLS // WIDE, teacher_chunk, 0)
    pl.semaphore_wait(barrier, 25)

    def pack(s):
        for j in range(32):
            nb[s, k, j : j + 1, :] = wide[0:1, j * LANES : (j + 1) * LANES]

    def near_send(s):
        for d in range(1, 8):
            remote(nb.at[s, k], nb.at[s, k], nb_s.at[s], nb_r.at[s], near(d)).start()

    def near_wait(s):
        await_bytes(nb.at[s, pl.ds(0, 7)], nb_r.at[s])

    def far_send(s):
        fsrc[s] = jnp.sum(nb[s], axis=0)
        remote(fsrc.at[s], fb.at[s], fb_s.at[s], fb_r.at[s], far()).start()

    def far_wait(s):
        remote(fsrc.at[s], fb.at[s], fb_s.at[s], fb_r.at[s], far()).wait()
        await_bytes(nb.at[s, pl.ds(0, 7)], nb_s.at[s])
        return fsrc[s] + fb[s]

    def unpack(v):
        for j in range(32):
            vrow[0:1, j * LANES : (j + 1) * LANES] = v[j : j + 1, :]

    def lanes_of(ref, i):
        blk = ref[i * LANES : (i + 1) * LANES, :]
        return jnp.sum(blk.T, axis=0, keepdims=True)

    def rows_of(v):
        return jnp.broadcast_to(v, (LANES, LANES)).T

    def x_send(buf, s):
        for d in range(1, NX):
            remote(buf.at[x], buf.at[x], xb_s.at[s], xb_r.at[s], along_x(d)).start()

    def x_wait(buf, s):
        await_bytes(buf.at[pl.ds(0, 3)], xb_r.at[s])
        await_bytes(buf.at[pl.ds(0, 3)], xb_s.at[s])
        return jnp.sum(buf[...], axis=0)

    def z_send(buf, s, value):
        buf[gz] = value
        for d in range(1, 16):
            remote(buf.at[gz], buf.at[gz], zb_s.at[s], zb_r.at[s], ring(d)).start()

    def z_wait(buf, s):
        await_bytes(buf.at[pl.ds(0, 15)], zb_r.at[s])
        await_bytes(buf.at[pl.ds(0, 15)], zb_s.at[s])

    def row_pass(src, dst, col0, v0, chunks):
        def block(r, _):
            rows = ds(r * 64, 64)

            def step(i, a):
                q = src[rows, ds(col0 + i * CHUNK, CHUNK)] * vrow[0:1, ds(v0 + i * CHUNK, CHUNK)]
                for j in range(CHUNK // LANES):
                    a = a + q[:, j * LANES : (j + 1) * LANES]
                return a

            dst[rows, :] = lax.fori_loop(0, chunks, step, jnp.zeros((64, LANES), F32))
            return 0

        lax.fori_loop(0, ROWS // 64, block, 0)

    half0 = zh * HALF

    def half_rows(s):
        row_pass(kexp, acc, half0, half0, HALF // CHUNK)
        row_pass(kp, accp, 0, half0, HALF // CHUNK)
        for i in range(3):
            xb[s, x, zh, 0:1, i * LANES : (i + 1) * LANES] = lanes_of(acc, i)
            xb[s, x, 1 - zh, 0:1, i * LANES : (i + 1) * LANES] = lanes_of(accp, i)

    def half_cols(s):
        def step(i, _):
            def rows_step(r, sums):
                for q in range(2):
                    rows = ds(r * 16 + q * 8, 8)
                    f = ub[rows, :]
                    g = ubp[rows, :]
                    sums = tuple(
                        sums[j]
                        + kexp[rows, ds(half0 + i * WIDE + j * LANES, LANES)] * f
                        + kp[rows, ds(i * WIDE + j * LANES, LANES)] * g
                        for j in range(8)
                    )
                return sums

            zero = jnp.zeros((8, LANES), F32)
            sums = lax.fori_loop(0, ROWS // 16, rows_step, (zero,) * 8)
            sums = [jnp.sum(v, axis=0, keepdims=True) for v in sums]
            nbh[s, k, ds(i * 8, 8), :] = jnp.concatenate(sums, axis=0)
            return 0

        lax.fori_loop(0, HALF // WIDE, step, 0)
        for d in range(1, 8):
            remote(nbh.at[s, k], nbh.at[s, k], nh_s.at[s], nh_r.at[s], near(d)).start()

    def half_scale(s):
        await_bytes(nbh.at[s, pl.ds(0, 7)], nh_r.at[s])
        await_bytes(nbh.at[s, pl.ds(0, 7)], nh_s.at[s])
        v = 1.0 / (PROTOS * jnp.sum(nbh[s], axis=0))
        for j in range(16):
            vrow[0:1, ds(half0 + j * LANES, LANES)] = v[j : j + 1, :]
        return v

    def rs_x_send(s, src, dst):
        for d in range(1, NX):
            rows = ds(((x + d) % NX) * 96, 96)
            remote(src.at[rows], dst.at[d - 1], x_s.at[s], x_r.at[s], along_x(d)).start()

    def rs_z_send(s, src, xr, zs, zr):
        await_bytes(xr, x_r.at[s])
        red = src[ds(x * 96, 96), :] + xr[0] + xr[1] + xr[2]
        zs[...] = red.reshape(SHARDS, OWN, DIM)
        for j in range(SHARDS):
            @pl.when(z != j + 1)
            def _():
                remote(zs.at[j], zr.at[z], z_s.at[s], z_r.at[s], at_z(j + 1)).start()

    owner = jnp.logical_and(z >= 1, z <= SHARDS)

    def rs_z_wait(s, zs, zr):
        await_bytes(zr.at[pl.ds(0, 7)], z_r.at[s])
        zr[z] = zs[z - 1]
        return jnp.sum(zr[...], axis=0)

    def rs_sent(s, xr, zs):
        await_bytes(xr, x_s.at[s])

        @pl.when(owner)
        def _():
            await_bytes(zs.at[pl.ds(0, SHARDS - 1)], z_s.at[s])

        @pl.when(jnp.logical_not(owner))
        def _():
            await_bytes(zs, z_s.at[s])

    def ag_z_send(s, full):
        ref = full.at[x, ds((z - 1) * OWN, OWN)]
        for d in range(1, NZ):
            remote(ref, ref, az_s.at[s], az_r.at[s], at_z((z + d) % NZ)).start()

    def ag_x_send(s, full):
        @pl.when(owner)
        def _():
            await_bytes(full.at[0, pl.ds(0, (SHARDS - 1) * OWN)], az_r.at[s])

        @pl.when(jnp.logical_not(owner))
        def _():
            await_bytes(full.at[0], az_r.at[s])

        for d in range(1, NX):
            remote(full.at[x], full.at[x], ax_s.at[s], ax_r.at[s], along_x(d)).start()

    def ag_wait(s, full):
        await_bytes(full.at[pl.ds(0, 3)], ax_r.at[s])
        await_bytes(full.at[pl.ds(0, 3)], ax_s.at[s])

        @pl.when(owner)
        def _():
            for d in range(1, NZ):
                await_bytes(full.at[0, pl.ds(0, OWN)], az_s.at[s])

        return full[...].reshape(ROWS, DIM)

    near_send(0)
    loads[1].wait()
    loads[2].wait()
    part[...] = lax.dot_general(
        hidden[...], w_last[...], (((0,), (0,)), ((), ())), preferred_element_type=F32
    )
    rs_x_send(0, part, xrecv)
    loads[3].wait()

    def student_cols(i, _):
        cols = ds(i * CHUNK, CHUNK)
        f = sp[:, cols].astype(F32)
        sc = lax.rsqrt(jnp.sum(f * f, axis=0, keepdims=True) + EPS)
        cscale[0:1, cols] = sc
        scols[:, cols] = (f * sc).astype(BF16)
        return 0

    lax.fori_loop(0, NCHUNK, student_cols, 0)
    near_wait(0)
    far_send(0)

    teach = remote(trows.at[ds(x * 96, 96)], tpr.at[x], mi_s, mi_r, mirror())
    teach.start()
    unpack(1.0 / (PROTOS * far_wait(0)))
    row_pass(kexp, acc, 0, 0, NCHUNK)
    for i in range(3):
        xb1[x, 0:1, i * LANES : (i + 1) * LANES] = lanes_of(acc, i)
    x_send(xb1, 0)
    teach.wait()
    for d in range(1, NX):
        remote(tpr.at[x], tpr.at[x], tx_s, tx_r, along_x(d)).start()
    z_send(zb1, 0, x_wait(xb1, 0))
    rs_z_send(0, part, xrecv, zsrc, zrecv)
    await_bytes(tpr.at[pl.ds(0, 3)], tx_r)
    await_bytes(tpr.at[pl.ds(0, 3)], tx_s)

    def partner_chunk(i, _):
        cols = ds(half0 + i * WIDE, WIDE)
        rows = tpr[...].reshape(ROWS, DIM)
        kp[:, ds(i * WIDE, WIDE)] = jnp.exp(
            25.0 * jnp.dot(rows, tp[:, cols], preferred_element_type=F32)
        )
        return 0

    lax.fori_loop(0, HALF // WIDE, partner_chunk, 0)

    def crop_scale(total_):
        return 1.0 / (CROPS * total_)

    def set_u(dst, v):
        for i in range(3):
            dst[i * LANES : (i + 1) * LANES, :] = rows_of(v[:, i * LANES : (i + 1) * LANES])

    z_wait(zb1, 0)
    set_u(ub, crop_scale(jnp.sum(zb1[pl.ds(zh * NZ, NZ)], axis=0)))
    set_u(ubp, crop_scale(jnp.sum(zb1[pl.ds((1 - zh) * NZ, NZ)], axis=0)))

    half_cols(0)
    half_scale(0)
    half_rows(0)
    x_send(xb.at[0], 1)

    @pl.when(owner)
    def _():
        bott = rs_z_wait(0, zsrc, zrecv)
        sc = lax.rsqrt(jnp.sum(bott * bott, axis=1, keepdims=True) + EPS)
        u = bott * sc
        unit[...] = u
        rscale[...] = jnp.broadcast_to(sc, (OWN, DIM))
        srows[x, ds((z - 1) * OWN, OWN), :] = u.astype(BF16)
        ag_z_send(0, srows)

    z_send(zb.at[0], 1, x_wait(xb.at[0], 1))
    rs_sent(0, xrecv, zsrc)
    ag_x_send(0, srows)
    z_wait(zb.at[0], 1)

    def of_group(s, g):
        return crop_scale(jnp.sum(zb[s, :, g], axis=0))

    set_u(ub, of_group(0, zh))
    set_u(ubp, of_group(0, 1 - zh))

    half_cols(1)
    ag_wait(0, srows)
    sacc[...] = jnp.zeros_like(sacc)

    def student_chunk(i, _):
        cols = ds(i * CHUNK, CHUNK)
        rows = srows[...].reshape(ROWS, DIM)
        e = jnp.exp(10.0 * jnp.dot(rows, scols[:, cols], preferred_element_type=F32))
        sexp[:, cols] = e
        a = sacc[...]
        for j in range(CHUNK // LANES):
            a = a + e[:, j * LANES : (j + 1) * LANES]
        sacc[...] = a
        return 0

    lax.fori_loop(0, NCHUNK, student_chunk, 0)
    vh[zh] = half_scale(1)
    v_copy = remote(vh.at[zh], vh.at[zh], vh_s, vh_r, far())
    v_copy.start()
    half_rows(1)
    x_send(xb.at[1], 2)
    for i in range(3):
        xbs[x, 0:1, i * LANES : (i + 1) * LANES] = lanes_of(sacc, i)
    x_send(xbs, 3)
    z_send(zb.at[1], 2, x_wait(xb.at[1], 2))
    zbs[z] = x_wait(xbs, 3)
    for d in range(1, NZ):
        remote(zbs.at[z], zbs.at[z], zb_s.at[3], zb_r.at[3], at_z((z + d) % NZ)).start()
    rowg[...] = jnp.zeros_like(rowg)
    v_copy.wait()
    for h in range(2):
        for j in range(16):
            at = h * HALF + j * LANES
            vrow[0:1, at : at + LANES] = vh[h, j : j + 1, :]
    gain = PROTOS / 128 * 10.0
    await_bytes(zbs.at[pl.ds(0, 7)], zb_r.at[3])
    await_bytes(zbs.at[pl.ds(0, 7)], zb_s.at[3])
    set_u(sacc, gain / jnp.sum(zbs[...], axis=0))
    z_wait(zb.at[1], 2)
    set_u(ub, (gain * CROPS) * of_group(1, zh))

    def c_copy(i):
        cols = ds(i * CHUNK, CHUNK)
        return remote(
            colall.at[:, 1 - c, :, cols], crecv.at[:, :, cols], c_s.at[i], c_r.at[i], core()
        )

    def y_copy(i, d):
        cols = ds(i * CHUNK, CHUNK)
        return remote(
            ysend.at[(y + d) % NY, :, :, cols], yrecv.at[d - 1, :, :, cols],
            y_s.at[i, d - 1], y_r.at[i, d - 1], along_y(d),
        )

    def zh_copy(i):
        cols = ds(i * CHUNK, CHUNK)
        return remote(zhsend.at[:, cols], zhrecv.at[:, cols], zh_s.at[i], zh_r.at[i], far())

    def y_send(i):
        cols = ds(i * CHUNK, CHUNK)
        c_copy(i).wait()
        for g in range(NY):
            for h in range(2):
                s = colall[h * NY + g, c, :, cols] + crecv[h * NY + g, :, cols]
                crecv[h * NY + g, :, cols] = s
                ysend[g, h, :, cols] = s.astype(BF16)
        for d in range(1, NY):
            y_copy(i, d).start()

    def zh_send(i, _):
        cols = ds(i * CHUNK, CHUNK)
        for d in range(1, NY):
            y_copy(i, d).wait()

        def over_y(h):
            s = crecv[h * NY + y, :, cols]
            for d in range(1, NY):
                s = s + yrecv[d - 1, h, :, cols].astype(F32)
            return s

        total[:, cols] = over_y(zh)
        zhsend[:, cols] = over_y(1 - zh).astype(BF16)
        zh_copy(i).start()
        return 0

    def grad_chunk(i, _):
        cols = ds(i * CHUNK, CHUNK)
        v = vrow[0:1, cols]
        pieces = []
        for j in range(CHUNK // LANES):
            lane = ds(i * CHUNK + j * LANES, LANES)
            vj = v[:, j * LANES : (j + 1) * LANES]
            pieces.append(
                (sexp[:, lane] * sacc[...] - (kexp[:, lane] * vj) * ub[...]).astype(BF16)
            )
        lg = jnp.concatenate(pieces, axis=1)
        lgs[:, cols] = lg
        rowg[...] += lax.dot_general(
            lg, scols[:, cols], (((1,), (1,)), ((), ())), preferred_element_type=F32
        )
        return 0

    def column_chunk(i, _):
        cols = ds(i * CHUNK, CHUNK)
        rows = srows[...].reshape(ROWS, DIM)
        colg = lax.dot_general(
            rows, lgs[:, cols], (((0,), (0,)), ((), ())), preferred_element_type=F32
        )
        colall[:, :, :, cols] = colg.reshape(8, 2, OWN, CHUNK)
        c_copy(i).start()
        un = sp[:, cols].astype(F32) * cscale[0:1, cols]
        wide[0:1, cols] = jnp.sum(un * colg, axis=0, keepdims=True)
        return 0

    def y_sends(i, _):
        y_send(i)
        return 0

    lax.fori_loop(0, NCHUNK, grad_chunk, 0)
    rs_x_send(1, rowg, rxrecv)
    lax.fori_loop(0, NCHUNK, column_chunk, 0)
    pack(1)
    near_send(1)
    rs_z_send(1, rowg, rxrecv, rzsrc, rzrecv)
    lax.fori_loop(0, NCHUNK, y_sends, 0)
    near_wait(1)
    far_send(1)
    lax.fori_loop(0, ZH0, zh_send, 0)

    @pl.when(owner)
    def _():
        g = rs_z_wait(1, rzsrc, rzrecv)
        u = unit[...]
        dot = jnp.sum(u * g, axis=1, keepdims=True)
        brows[x, ds((z - 1) * OWN, OWN), :] = (rscale[...] * (g - u * dot)).astype(BF16)
        ag_z_send(1, brows)

    lax.fori_loop(ZH0, ZH1, zh_send, 0)
    ag_x_send(1, brows)
    lax.fori_loop(ZH1, NCHUNK, zh_send, 0)
    unpack(far_wait(1))
    bg = ag_wait(1, brows)
    wg = jnp.dot(hidden[...], bg, preferred_element_type=F32)
    wsrc[...] = wg.reshape(8, 8, DIM)
    for d in range(1, 8):
        remote(wsrc.at[(k + d) % 8], wrecv.at[k], w_s, w_r, near(d)).start()

    def finish(i, _):
        cols = ds(i * CHUNK, CHUNK)
        zh_copy(i).wait()
        s = total[:, cols] + zhrecv[:, cols].astype(F32)
        sc = cscale[0:1, cols]
        un = sp[ds(b * OWN, OWN), cols].astype(F32) * sc
        total[:, cols] = sc * (s - un * vrow[0:1, cols])
        pltpu.make_async_copy(total.at[:, cols], out_pg.at[:, cols], out_s.at[i]).start()
        return 0

    await_bytes(wrecv.at[pl.ds(0, 7)], w_r)
    wrecv[k] = wsrc[k]
    wfsrc[...] = jnp.sum(wrecv[...], axis=0)
    wf = remote(wfsrc, wfrecv, wf_s, wf_r, far())
    wf.start()
    lax.fori_loop(0, NCHUNK, finish, 0)
    rs_sent(1, rxrecv, rzsrc)
    await_bytes(wsrc.at[pl.ds(0, 7)], w_s)
    wf.wait()
    wfull[k] = wfsrc[...] + wfrecv[...]
    for d in range(1, 8):
        remote(wfull.at[k], wfull.at[k], wg_s, wg_r, near(d)).start()
    await_bytes(wfull.at[pl.ds(0, 7)], wg_r)
    await_bytes(wfull.at[pl.ds(0, 7)], wg_s)
    last = pltpu.make_async_copy(wfull, out_wg, out_s.at[NCHUNK])
    last.start()

    def sent(i, _):
        cols = ds(i * CHUNK, CHUNK)
        pltpu.make_async_copy(total.at[:, cols], out_pg.at[:, cols], out_s.at[i]).wait()
        return 0

    lax.fori_loop(0, NCHUNK, sent, 0)
    last.wait()


def move(pg_in, wg_in, pg, wg, pg_buf, wg_buf, sem):
    stages = [(pg_in, pg_buf, pg), (wg_in, wg_buf, wg)]
    loads = [pltpu.make_async_copy(src, buf, sem.at[i]) for i, (src, buf, _) in enumerate(stages)]
    stores = [pltpu.make_async_copy(buf, dst, sem.at[2 + i]) for i, (_, buf, dst) in enumerate(stages)]
    for copy in loads:
        copy.start()
    for i in (1, 0):
        loads[i].wait()
        stores[i].start()
    for copy in stores:
        copy.wait()


def per_device(hidden, w_last, student_protos, teacher_bneck, teacher_protos):
    vm = pltpu.VMEM
    dma = pltpu.SemaphoreType.DMA
    scratch = [
        vm((64, ROWS), BF16), vm((64, DIM), BF16), vm((DIM, COLS), BF16), vm((ROWS, DIM), BF16),
        vm((DIM, COLS), BF16), dma((8,)), dma((NCHUNK + 1,)),
        vm((ROWS, COLS), F32), vm((ROWS, COLS), F32), vm((DIM, COLS), BF16), vm((8, COLS), F32),
        vm((ROWS, DIM), BF16), vm((ROWS, LANES), F32), vm((8, COLS), F32), vm((8, COLS), F32),
        vm((ROWS, LANES), F32), vm((ROWS, LANES), F32), vm((ROWS, DIM), F32),
        vm((3, 96, DIM), F32), vm((SHARDS, OWN, DIM), F32), vm((NZ, OWN, DIM), F32),
        vm((OWN, DIM), F32), vm((OWN, DIM), F32), vm((NX, 96, DIM), BF16), vm((ROWS, DIM), F32),
        vm((3, 96, DIM), F32), vm((SHARDS, OWN, DIM), F32), vm((NZ, OWN, DIM), F32),
        vm((NX, 96, DIM), BF16),
        vm((2, 8, 32, LANES), F32), vm((2, 32, LANES), F32), vm((2, 32, LANES), F32),
        vm((2, 8, 16, LANES), F32), vm((2, 16, LANES), F32),
        vm((NX, 1, ROWS), F32), vm((16, 1, ROWS), F32), vm((2, NX, 2, 1, ROWS), F32),
        vm((2, 16, 2, 1, ROWS), F32), vm((NX, 1, ROWS), F32), vm((NZ, 1, ROWS), F32),
        vm((ROWS, HALF), F32), vm((NX, 96, DIM), BF16), vm((ROWS, LANES), F32),
        vm((ROWS, LANES), F32),
        vm((ROWS, COLS), BF16), vm((8, 2, OWN, COLS), F32), vm((8, OWN, COLS), F32), vm((NY, 2, OWN, COLS), BF16),
        vm((3, 2, OWN, COLS), BF16), vm((OWN, COLS), BF16), vm((OWN, COLS), BF16),
        vm((OWN, COLS), F32),
        vm((8, 8, DIM), F32), vm((8, 8, DIM), F32), vm((8, DIM), F32), vm((8, DIM), F32),
        vm((8, 8, DIM), F32),
        dma((2,)), dma((2,)), dma((2,)), dma((2,)), dma((2,)), dma((2,)), dma, dma,
        dma((4,)), dma((4,)), dma((4,)), dma((4,)), dma, dma, dma, dma,
        dma((2,)), dma((2,)), dma((2,)), dma((2,)), dma((2,)), dma((2,)), dma((2,)), dma((2,)),
        dma((NCHUNK,)), dma((NCHUNK,)), dma((NCHUNK, 3)), dma((NCHUNK, 3)),
        dma((NCHUNK,)), dma((NCHUNK,)), dma, dma, dma, dma, dma, dma,
    ]
    spec = pl.BlockSpec(memory_space=pl.ANY)
    shapes = (
        jax.ShapeDtypeStruct((OWN, COLS), F32),
        jax.ShapeDtypeStruct((8, 8, DIM), F32),
    )
    results = pl.pallas_call(
        kernel,
        out_shape=shapes,
        in_specs=[spec] * 5,
        out_specs=(spec, spec),
        scratch_shapes=scratch,
        compiler_params=pltpu.CompilerParams(
            collective_id=0, has_side_effects=True, vmem_limit_bytes=60 * 1024 * 1024
        ),
        name="dino_head",
    )(hidden.T, w_last, student_protos, teacher_bneck, teacher_protos)
    proto_grad, weight_grad = pl.pallas_call(
        move,
        out_shape=shapes,
        in_specs=[spec] * 2,
        out_specs=(spec, spec),
        scratch_shapes=[vm((OWN, COLS), F32), vm((8, 8, DIM), F32), dma((4,))],
        name="move_results",
    )(*results)
    return proto_grad, weight_grad.reshape(64, DIM)


def solution(mesh):
    placed = (
        P("batch", "proto"),
        P("proto", None),
        P(None, "proto"),
        P("batch", None),
        P(None, "proto"),
    )
    return jax.shard_map(
        per_device,
        mesh=mesh,
        in_specs=placed,
        out_specs=(P("batch", "proto"), P("proto", None)),
        check_vma=False,
    )
```

```python
import functools

import jax
import jax.numpy as jnp
from jax import lax
from jax.experimental import pallas as pl
from jax.experimental.pallas import tpu as pltpu
from jax.sharding import PartitionSpec as P

PROTOS = 131072
CROPS = 6144
ITERS = 3
EPS = 1e-06
F32 = jnp.float32
BF16 = jnp.bfloat16
MESH = pl.DeviceIdType.MESH

ROWS = 384
COLS = 4096
DIM = 256
CHUNK = 512
WIDE = 1024
NCHUNK = COLS // CHUNK
HALF = COLS // 2
LANES = 128
NX, NZ, NY = 4, 8, 4
OWN = 16
SHARDS = 6


def ds(start, size):
    return pl.ds(pl.multiple_of(start, size), size)


def kernel(
    hidden_in, w_in, sp_in, tb_in, tp_in, out_pg, out_wg,
    hidden, w_last, sp, tb, tp, in_s, out_s,
    kexp, sexp, scols, cscale, trows, ub, wide, vrow, acc, sacc, part,
    xrecv, zsrc, zrecv, unit, rscale, srows, rowg, rxrecv, rzsrc, rzrecv, brows,
    nb, fsrc, fb, nbh, vh, xb1, zb1, xb, zb, xbs, zbs, kp, tpr, ubp, accp, lgs, colall, crecv, ysend, yrecv, zhsend, zhrecv, total,
    wsrc, wrecv, wfsrc, wfrecv, wfull,
    nb_s, nb_r, fb_s, fb_r, nh_s, nh_r, vh_s, vh_r, xb_s, xb_r, zb_s, zb_r,
    mi_s, mi_r, tx_s, tx_r, x_s, x_r, z_s, z_r, az_s, az_r, ax_s, ax_r,
    c_s, c_r, y_s, y_r, zh_s, zh_r, w_s, w_r, wf_s, wf_r, wg_s, wg_r,
):
    b = lax.axis_index("batch")
    p = lax.axis_index("proto")
    zh = b // 8
    k = b % 8
    y = k // 2
    c = b % 2
    z = p // NX
    x = p % NX

    def near(d):
        return {"batch": zh * 8 + (k + d) % 8, "proto": p}

    def far():
        return {"batch": (1 - zh) * 8 + k, "proto": p}

    def core():
        return {"batch": zh * 8 + y * 2 + (1 - c), "proto": p}

    def along_y(d):
        return {"batch": zh * 8 + ((y + d) % NY) * 2 + c, "proto": p}

    def along_x(d):
        return {"batch": b, "proto": z * NX + (x + d) % NX}

    def at_z(j):
        return {"batch": b, "proto": j * NX + x}

    gz = zh * NZ + z

    def ring(d):
        g = (gz + d) % 16
        return {"batch": (g // NZ) * 8 + k, "proto": (g % NZ) * NX + x}

    def mirror():
        return {"batch": (1 - zh) * 8 + k, "proto": (NZ - 1 - z) * NX + x}

    def remote(src, dst, ss, rs, dev):
        return pltpu.make_async_remote_copy(
            src_ref=src, dst_ref=dst, send_sem=ss, recv_sem=rs, device_id=dev, device_id_type=MESH
        )

    def await_bytes(ref, sem):
        pltpu.make_async_copy(ref, ref, sem).wait()

    def load(src, dst, i):
        return pltpu.make_async_copy(src, dst, in_s.at[i])

    def tp_load(i):
        cols = ds(i * WIDE, WIDE)
        return load(tp_in.at[:, cols], tp.at[:, cols], i)

    loads = [load(tb_in, tb, 4), load(hidden_in, hidden, 5), load(w_in, w_last, 6), load(sp_in, sp, 7)]
    loads[0].start()
    for i in range(COLS // WIDE):
        tp_load(i).start()
    for copy in loads[1:]:
        copy.start()

    barrier = pltpu.get_barrier_semaphore()

    def greet(dev):
        pl.semaphore_signal(barrier, inc=1, device_id=dev, device_id_type=MESH)

    for d in range(1, 8):
        greet(near(d))
    for d in range(1, NX):
        greet(along_x(d))
    for d in range(1, 16):
        greet(ring(d))

    loads[0].wait()
    t = tb[...].astype(F32)
    trows[...] = (t * lax.rsqrt(jnp.sum(t * t, axis=1, keepdims=True) + EPS)).astype(BF16)

    def store_sums(s, i, sums):
        nb[s, k, ds(i * 8, 8), :] = jnp.concatenate(sums, axis=0)

    def teacher_chunk(i, _):
        cols = ds(i * WIDE, WIDE)
        tp_load(i).wait()
        f = tp[:, cols].astype(F32)
        tc = (f * lax.rsqrt(jnp.sum(f * f, axis=0, keepdims=True) + EPS)).astype(BF16)
        e = jnp.exp(25.0 * jnp.dot(trows[...], tc, preferred_element_type=F32))
        tp[:, cols] = tc
        kexp[:, cols] = e
        sums = jnp.sum(e, axis=0, keepdims=True)
        store_sums(0, i, [sums[:, j * LANES : (j + 1) * LANES] for j in range(8)])
        return 0

    lax.fori_loop(0, COLS // WIDE, teacher_chunk, 0)
    pl.semaphore_wait(barrier, 25)

    def pack(s):
        for j in range(32):
            nb[s, k, j : j + 1, :] = wide[0:1, j * LANES : (j + 1) * LANES]

    def near_send(s):
        for d in range(1, 8):
            remote(nb.at[s, k], nb.at[s, k], nb_s.at[s], nb_r.at[s], near(d)).start()

    def near_wait(s):
        await_bytes(nb.at[s, pl.ds(0, 7)], nb_r.at[s])

    def far_send(s):
        fsrc[s] = jnp.sum(nb[s], axis=0)
        remote(fsrc.at[s], fb.at[s], fb_s.at[s], fb_r.at[s], far()).start()

    def far_wait(s):
        remote(fsrc.at[s], fb.at[s], fb_s.at[s], fb_r.at[s], far()).wait()
        await_bytes(nb.at[s, pl.ds(0, 7)], nb_s.at[s])
        return fsrc[s] + fb[s]

    def unpack(v):
        for j in range(32):
            vrow[0:1, j * LANES : (j + 1) * LANES] = v[j : j + 1, :]

    def lanes_of(ref, i):
        blk = ref[i * LANES : (i + 1) * LANES, :]
        return jnp.sum(blk.T, axis=0, keepdims=True)

    def rows_of(v):
        return jnp.broadcast_to(v, (LANES, LANES)).T

    def x_send(buf, s):
        for d in range(1, NX):
            remote(buf.at[x], buf.at[x], xb_s.at[s], xb_r.at[s], along_x(d)).start()

    def x_wait(buf, s):
        await_bytes(buf.at[pl.ds(0, 3)], xb_r.at[s])
        await_bytes(buf.at[pl.ds(0, 3)], xb_s.at[s])
        return jnp.sum(buf[...], axis=0)

    def z_send(buf, s, value):
        buf[gz] = value
        for d in range(1, 16):
            remote(buf.at[gz], buf.at[gz], zb_s.at[s], zb_r.at[s], ring(d)).start()

    def z_wait(buf, s):
        await_bytes(buf.at[pl.ds(0, 15)], zb_r.at[s])
        await_bytes(buf.at[pl.ds(0, 15)], zb_s.at[s])

    def row_pass(src, dst, col0, v0, chunks):
        def block(r, _):
            rows = ds(r * 64, 64)

            def step(i, a):
                q = src[rows, ds(col0 + i * CHUNK, CHUNK)] * vrow[0:1, ds(v0 + i * CHUNK, CHUNK)]
                for j in range(CHUNK // LANES):
                    a = a + q[:, j * LANES : (j + 1) * LANES]
                return a

            dst[rows, :] = lax.fori_loop(0, chunks, step, jnp.zeros((64, LANES), F32))
            return 0

        lax.fori_loop(0, ROWS // 64, block, 0)

    half0 = zh * HALF

    def half_rows(s):
        row_pass(kexp, acc, half0, half0, HALF // CHUNK)
        row_pass(kp, accp, 0, half0, HALF // CHUNK)
        for i in range(3):
            xb[s, x, zh, 0:1, i * LANES : (i + 1) * LANES] = lanes_of(acc, i)
            xb[s, x, 1 - zh, 0:1, i * LANES : (i + 1) * LANES] = lanes_of(accp, i)

    def half_cols(s):
        def step(i, _):
            def rows_step(r, sums):
                for q in range(2):
                    rows = ds(r * 16 + q * 8, 8)
                    f = ub[rows, :]
                    g = ubp[rows, :]
                    sums = tuple(
                        sums[j]
                        + kexp[rows, ds(half0 + i * WIDE + j * LANES, LANES)] * f
                        + kp[rows, ds(i * WIDE + j * LANES, LANES)] * g
                        for j in range(8)
                    )
                return sums

            zero = jnp.zeros((8, LANES), F32)
            sums = lax.fori_loop(0, ROWS // 16, rows_step, (zero,) * 8)
            sums = [jnp.sum(v, axis=0, keepdims=True) for v in sums]
            nbh[s, k, ds(i * 8, 8), :] = jnp.concatenate(sums, axis=0)
            return 0

        lax.fori_loop(0, HALF // WIDE, step, 0)
        for d in range(1, 8):
            remote(nbh.at[s, k], nbh.at[s, k], nh_s.at[s], nh_r.at[s], near(d)).start()

    def half_scale(s):
        await_bytes(nbh.at[s, pl.ds(0, 7)], nh_r.at[s])
        await_bytes(nbh.at[s, pl.ds(0, 7)], nh_s.at[s])
        v = 1.0 / (PROTOS * jnp.sum(nbh[s], axis=0))
        for j in range(16):
            vrow[0:1, ds(half0 + j * LANES, LANES)] = v[j : j + 1, :]
        return v

    def rs_x_send(s, half, src, dst):
        for d in range(1, NX):
            rows = ds(half * 192 + ((x + d) % NX) * 48, 48)
            remote(
                src.at[rows], dst.at[half, d - 1], x_s.at[s, half], x_r.at[s, half], along_x(d)
            ).start()

    def rs_z_send(s, half, src, xr, zs, zr):
        await_bytes(xr.at[half], x_r.at[s, half])
        red = src[ds(half * 192 + x * 48, 48), :] + xr[half, 0] + xr[half, 1] + xr[half, 2]
        zs[half] = red.reshape(3, OWN, DIM)
        for jj in range(3):
            to = 2 * jj + half + 1

            @pl.when(z != to)
            def _():
                remote(zs.at[half, jj], zr.at[z], z_s.at[s], z_r.at[s], at_z(to)).start()

    owner = jnp.logical_and(z >= 1, z <= SHARDS)
    my_half = (z - 1) % 2
    my_rows = ds((z - 1) // 2 * OWN, OWN)

    def rs_z_wait(s, zs, zr):
        await_bytes(zr.at[pl.ds(0, 7)], z_r.at[s])
        zr[z] = zs[my_half, (z - 1) // 2]
        return jnp.sum(zr[...], axis=0)

    def rs_sent(s, xr, zr):
        for half in range(2):
            await_bytes(xr.at[half], x_s.at[s, half])

        @pl.when(owner)
        def _():
            await_bytes(zr.at[pl.ds(0, SHARDS - 1)], z_s.at[s])

        @pl.when(jnp.logical_not(owner))
        def _():
            await_bytes(zr.at[pl.ds(0, SHARDS)], z_s.at[s])

    def ag_z_send(s, full):
        ref = full.at[my_half, x, my_rows]
        for d in range(1, NZ):
            remote(ref, ref, az_s.at[s], az_r.at[s, z - 1], at_z((z + d) % NZ)).start()

    def ag_x_send(s, full):
        for j in range(SHARDS):
            @pl.when(z != j + 1)
            def _():
                await_bytes(full.at[j % 2, x, pl.ds(j // 2 * OWN, OWN)], az_r.at[s, j])

        for d in range(1, NX):
            remote(full.at[:, x], full.at[:, x], ax_s.at[s], ax_r.at[s], along_x(d)).start()

    def ag_wait(s, full):
        await_bytes(full.at[:, pl.ds(0, 3)], ax_r.at[s])
        await_bytes(full.at[:, pl.ds(0, 3)], ax_s.at[s])

        @pl.when(owner)
        def _():
            for d in range(1, NZ):
                await_bytes(full.at[0, 0, pl.ds(0, OWN)], az_s.at[s])

        return full[...].reshape(ROWS, DIM)

    near_send(0)
    loads[1].wait()
    loads[2].wait()
    part[...] = lax.dot_general(
        hidden[...], w_last[...], (((0,), (0,)), ((), ())), preferred_element_type=F32
    )
    rs_x_send(0, 0, part, xrecv)
    rs_x_send(0, 1, part, xrecv)
    loads[3].wait()

    def student_cols(i, _):
        cols = ds(i * CHUNK, CHUNK)
        f = sp[:, cols].astype(F32)
        sc = lax.rsqrt(jnp.sum(f * f, axis=0, keepdims=True) + EPS)
        cscale[0:1, cols] = sc
        scols[:, cols] = (f * sc).astype(BF16)
        return 0

    lax.fori_loop(0, NCHUNK, student_cols, 0)
    near_wait(0)
    far_send(0)

    teach = remote(trows.at[ds(x * 96, 96)], tpr.at[x], mi_s, mi_r, mirror())
    teach.start()
    unpack(1.0 / (PROTOS * far_wait(0)))
    row_pass(kexp, acc, 0, 0, NCHUNK)
    for i in range(3):
        xb1[x, 0:1, i * LANES : (i + 1) * LANES] = lanes_of(acc, i)
    x_send(xb1, 0)
    teach.wait()
    for d in range(1, NX):
        remote(tpr.at[x], tpr.at[x], tx_s, tx_r, along_x(d)).start()
    z_send(zb1, 0, x_wait(xb1, 0))
    rs_z_send(0, 0, part, xrecv, zsrc, zrecv)
    rs_z_send(0, 1, part, xrecv, zsrc, zrecv)
    await_bytes(tpr.at[pl.ds(0, 3)], tx_r)
    await_bytes(tpr.at[pl.ds(0, 3)], tx_s)

    def partner_chunk(i, _):
        cols = ds(half0 + i * WIDE, WIDE)
        rows = tpr[...].reshape(ROWS, DIM)
        kp[:, ds(i * WIDE, WIDE)] = jnp.exp(
            25.0 * jnp.dot(rows, tp[:, cols], preferred_element_type=F32)
        )
        return 0

    lax.fori_loop(0, HALF // WIDE, partner_chunk, 0)

    def crop_scale(total_):
        return 1.0 / (CROPS * total_)

    def set_u(dst, v):
        for i in range(3):
            dst[i * LANES : (i + 1) * LANES, :] = rows_of(v[:, i * LANES : (i + 1) * LANES])

    z_wait(zb1, 0)
    set_u(ub, crop_scale(jnp.sum(zb1[pl.ds(zh * NZ, NZ)], axis=0)))
    set_u(ubp, crop_scale(jnp.sum(zb1[pl.ds((1 - zh) * NZ, NZ)], axis=0)))

    half_cols(0)
    half_scale(0)
    half_rows(0)
    x_send(xb.at[0], 1)

    @pl.when(owner)
    def _():
        bott = rs_z_wait(0, zsrc, zrecv)
        sc = lax.rsqrt(jnp.sum(bott * bott, axis=1, keepdims=True) + EPS)
        u = bott * sc
        unit[...] = u
        rscale[...] = jnp.broadcast_to(sc, (OWN, DIM))
        srows[my_half, x, my_rows, :] = u.astype(BF16)
        ag_z_send(0, srows)

    z_send(zb.at[0], 1, x_wait(xb.at[0], 1))
    rs_sent(0, xrecv, zrecv)
    ag_x_send(0, srows)
    z_wait(zb.at[0], 1)

    def of_group(s, g):
        return crop_scale(jnp.sum(zb[s, :, g], axis=0))

    set_u(ub, of_group(0, zh))
    set_u(ubp, of_group(0, 1 - zh))

    half_cols(1)
    ag_wait(0, srows)
    sacc[...] = jnp.zeros_like(sacc)

    def student_chunk(i, _):
        cols = ds(i * CHUNK, CHUNK)
        rows = srows[...].reshape(ROWS, DIM)
        e = jnp.exp(10.0 * jnp.dot(rows, scols[:, cols], preferred_element_type=F32))
        sexp[:, cols] = e
        a = sacc[...]
        for j in range(CHUNK // LANES):
            a = a + e[:, j * LANES : (j + 1) * LANES]
        sacc[...] = a
        return 0

    lax.fori_loop(0, NCHUNK, student_chunk, 0)
    vh[zh] = half_scale(1)
    v_copy = remote(vh.at[zh], vh.at[zh], vh_s, vh_r, far())
    v_copy.start()
    half_rows(1)
    x_send(xb.at[1], 2)
    for i in range(3):
        xbs[x, 0:1, i * LANES : (i + 1) * LANES] = lanes_of(sacc, i)
    x_send(xbs, 3)
    zb[1, gz] = x_wait(xb.at[1], 2)
    for d in range(1, 16):
        part_ref = zb.at[1, gz, (gz + d) % 16 // NZ]
        remote(part_ref, part_ref, zb_s.at[2], zb_r.at[2], ring(d)).start()
    zbs[z] = x_wait(xbs, 3)
    for d in range(1, NZ):
        remote(zbs.at[z], zbs.at[z], zb_s.at[3], zb_r.at[3], at_z((z + d) % NZ)).start()
    rowg[...] = jnp.zeros_like(rowg)
    v_copy.wait()
    for h in range(2):
        for j in range(16):
            at = h * HALF + j * LANES
            vrow[0:1, at : at + LANES] = vh[h, j : j + 1, :]
    gain = PROTOS / 128 * 10.0
    await_bytes(zbs.at[pl.ds(0, 7)], zb_r.at[3])
    await_bytes(zbs.at[pl.ds(0, 7)], zb_s.at[3])
    set_u(sacc, gain / jnp.sum(zbs[...], axis=0))
    await_bytes(zb.at[1, pl.ds(0, 15), zh], zb_r.at[2])
    await_bytes(zb.at[1, pl.ds(0, 15), zh], zb_s.at[2])
    set_u(ub, (gain * CROPS) * of_group(1, zh))

    def c_copy(i):
        cols = ds(i * CHUNK, CHUNK)
        return remote(
            colall.at[:, 1 - c, :, cols], crecv.at[:, :, cols], c_s.at[i], c_r.at[i], core()
        )

    def y_copy(i, d):
        cols = ds(i * CHUNK, CHUNK)
        return remote(
            ysend.at[(y + d) % NY, :, :, cols], yrecv.at[d - 1, :, :, cols],
            y_s.at[i, d - 1], y_r.at[i, d - 1], along_y(d),
        )

    def zh_copy(i):
        cols = ds(i * CHUNK, CHUNK)
        return remote(zhsend.at[:, cols], zhrecv.at[:, cols], zh_s.at[i], zh_r.at[i], far())

    def y_send(i):
        cols = ds(i * CHUNK, CHUNK)
        c_copy(i).wait()
        for g in range(NY):
            for h in range(2):
                s = colall[h * NY + g, c, :, cols] + crecv[h * NY + g, :, cols]
                crecv[h * NY + g, :, cols] = s
                ysend[g, h, :, cols] = s.astype(BF16)
        for d in range(1, NY):
            y_copy(i, d).start()

    def zh_send(i, _):
        cols = ds(i * CHUNK, CHUNK)
        for d in range(1, NY):
            y_copy(i, d).wait()

        def over_y(h):
            s = crecv[h * NY + y, :, cols]
            for d in range(1, NY):
                s = s + yrecv[d - 1, h, :, cols].astype(F32)
            return s

        total[:, cols] = over_y(zh)
        zhsend[:, cols] = over_y(1 - zh).astype(BF16)
        zh_copy(i).start()
        return 0

    def grad_half(half):
        rows = slice(half * 192, half * 192 + 192)

        def step(i, _):
            cols = ds(i * WIDE, WIDE)
            pieces = []
            for j in range(WIDE // LANES):
                lane = ds(i * WIDE + j * LANES, LANES)
                targets = (kexp[rows, lane] * vrow[0:1, lane]) * ub[rows, :]
                pieces.append((sexp[rows, lane] * sacc[rows, :] - targets).astype(BF16))
            lg = jnp.concatenate(pieces, axis=1)
            lgs[rows, cols] = lg
            rowg[rows, :] += lax.dot_general(
                lg, scols[:, cols], (((1,), (1,)), ((), ())), preferred_element_type=F32
            )
            return 0

        lax.fori_loop(0, COLS // WIDE, step, 0)
        rs_x_send(1, half, rowg, rxrecv)

    def column_chunk(i, _):
        cols = ds(i * CHUNK, CHUNK)
        rows = srows[...].reshape(ROWS, DIM)
        colg = lax.dot_general(
            rows, lgs[:, cols], (((0,), (0,)), ((), ())), preferred_element_type=F32
        )
        colall[:, :, :, cols] = colg.reshape(8, 2, OWN, CHUNK)
        c_copy(i).start()
        un = sp[:, cols].astype(F32) * cscale[0:1, cols]
        wide[0:1, cols] = jnp.sum(un * colg, axis=0, keepdims=True)
        return 0

    def y_sends(i, _):
        y_send(i)
        return 0

    grad_half(0)
    grad_half(1)
    lax.fori_loop(0, NCHUNK, column_chunk, 0)
    pack(1)
    near_send(1)
    rs_z_send(1, 0, rowg, rxrecv, rzsrc, rzrecv)
    rs_z_send(1, 1, rowg, rxrecv, rzsrc, rzrecv)
    lax.fori_loop(0, NCHUNK, y_sends, 0)
    near_wait(1)
    far_send(1)

    @pl.when(owner)
    def _():
        g = rs_z_wait(1, rzsrc, rzrecv)
        u = unit[...]
        dot = jnp.sum(u * g, axis=1, keepdims=True)
        brows[my_half, x, my_rows, :] = (rscale[...] * (g - u * dot)).astype(BF16)
        ag_z_send(1, brows)

    ag_x_send(1, brows)
    lax.fori_loop(0, NCHUNK, zh_send, 0)
    unpack(far_wait(1))
    bg = ag_wait(1, brows)
    wg = jnp.dot(hidden[...], bg, preferred_element_type=F32)
    wsrc[...] = wg.reshape(8, 8, DIM)
    for d in range(1, 8):
        remote(wsrc.at[(k + d) % 8], wrecv.at[k], w_s, w_r, near(d)).start()

    def finish(i, _):
        cols = ds(i * CHUNK, CHUNK)
        zh_copy(i).wait()
        s = total[:, cols] + zhrecv[:, cols].astype(F32)
        sc = cscale[0:1, cols]
        un = sp[ds(b * OWN, OWN), cols].astype(F32) * sc
        total[:, cols] = sc * (s - un * vrow[0:1, cols])
        pltpu.make_async_copy(total.at[:, cols], out_pg.at[:, cols], out_s.at[i]).start()
        return 0

    await_bytes(wrecv.at[pl.ds(0, 7)], w_r)
    wrecv[k] = wsrc[k]
    wfsrc[...] = jnp.sum(wrecv[...], axis=0)
    wf = remote(wfsrc, wfrecv, wf_s, wf_r, far())
    wf.start()
    lax.fori_loop(0, NCHUNK, finish, 0)
    rs_sent(1, rxrecv, rzrecv)
    await_bytes(wsrc.at[pl.ds(0, 7)], w_s)
    wf.wait()
    wfull[k] = wfsrc[...] + wfrecv[...]
    for d in range(1, 8):
        remote(wfull.at[k], wfull.at[k], wg_s, wg_r, near(d)).start()
    await_bytes(wfull.at[pl.ds(0, 7)], wg_r)
    await_bytes(wfull.at[pl.ds(0, 7)], wg_s)
    last = pltpu.make_async_copy(wfull, out_wg, out_s.at[NCHUNK])
    last.start()

    def sent(i, _):
        cols = ds(i * CHUNK, CHUNK)
        pltpu.make_async_copy(total.at[:, cols], out_pg.at[:, cols], out_s.at[i]).wait()
        return 0

    lax.fori_loop(0, NCHUNK, sent, 0)
    last.wait()


def move(pg_in, wg_in, pg, wg, pg_buf, wg_buf, sem):
    stages = [(pg_in, pg_buf, pg), (wg_in, wg_buf, wg)]
    loads = [pltpu.make_async_copy(src, buf, sem.at[i]) for i, (src, buf, _) in enumerate(stages)]
    stores = [pltpu.make_async_copy(buf, dst, sem.at[2 + i]) for i, (_, buf, dst) in enumerate(stages)]
    for copy in loads:
        copy.start()
    for i in (1, 0):
        loads[i].wait()
        stores[i].start()
    for copy in stores:
        copy.wait()


def per_device(hidden, w_last, student_protos, teacher_bneck, teacher_protos):
    vm = pltpu.VMEM
    dma = pltpu.SemaphoreType.DMA
    scratch = [
        vm((64, ROWS), BF16), vm((64, DIM), BF16), vm((DIM, COLS), BF16), vm((ROWS, DIM), BF16),
        vm((DIM, COLS), BF16), dma((8,)), dma((NCHUNK + 1,)),
        vm((ROWS, COLS), F32), vm((ROWS, COLS), F32), vm((DIM, COLS), BF16), vm((8, COLS), F32),
        vm((ROWS, DIM), BF16), vm((ROWS, LANES), F32), vm((8, COLS), F32), vm((8, COLS), F32),
        vm((ROWS, LANES), F32), vm((ROWS, LANES), F32), vm((ROWS, DIM), F32),
        vm((2, 3, 48, DIM), F32), vm((2, 3, OWN, DIM), F32), vm((NZ, OWN, DIM), F32),
        vm((OWN, DIM), F32), vm((OWN, DIM), F32), vm((2, NX, 48, DIM), BF16), vm((ROWS, DIM), F32),
        vm((2, 3, 48, DIM), F32), vm((2, 3, OWN, DIM), F32), vm((NZ, OWN, DIM), F32),
        vm((2, NX, 48, DIM), BF16),
        vm((2, 8, 32, LANES), F32), vm((2, 32, LANES), F32), vm((2, 32, LANES), F32),
        vm((2, 8, 16, LANES), F32), vm((2, 16, LANES), F32),
        vm((NX, 1, ROWS), F32), vm((16, 1, ROWS), F32), vm((2, NX, 2, 1, ROWS), F32),
        vm((2, 16, 2, 1, ROWS), F32), vm((NX, 1, ROWS), F32), vm((NZ, 1, ROWS), F32),
        vm((ROWS, HALF), F32), vm((NX, 96, DIM), BF16), vm((ROWS, LANES), F32),
        vm((ROWS, LANES), F32),
        vm((ROWS, COLS), BF16), vm((8, 2, OWN, COLS), F32), vm((8, OWN, COLS), F32), vm((NY, 2, OWN, COLS), BF16),
        vm((3, 2, OWN, COLS), BF16), vm((OWN, COLS), BF16), vm((OWN, COLS), BF16),
        vm((OWN, COLS), F32),
        vm((8, 8, DIM), F32), vm((8, 8, DIM), F32), vm((8, DIM), F32), vm((8, DIM), F32),
        vm((8, 8, DIM), F32),
        dma((2,)), dma((2,)), dma((2,)), dma((2,)), dma((2,)), dma((2,)), dma, dma,
        dma((4,)), dma((4,)), dma((4,)), dma((4,)), dma, dma, dma, dma,
        dma((2, 2)), dma((2, 2)), dma((2,)), dma((2,)), dma((2,)), dma((2, SHARDS)), dma((2,)), dma((2,)),
        dma((NCHUNK,)), dma((NCHUNK,)), dma((NCHUNK, 3)), dma((NCHUNK, 3)),
        dma((NCHUNK,)), dma((NCHUNK,)), dma, dma, dma, dma, dma, dma,
    ]
    spec = pl.BlockSpec(memory_space=pl.ANY)
    shapes = (
        jax.ShapeDtypeStruct((OWN, COLS), F32),
        jax.ShapeDtypeStruct((8, 8, DIM), F32),
    )
    results = pl.pallas_call(
        kernel,
        out_shape=shapes,
        in_specs=[spec] * 5,
        out_specs=(spec, spec),
        scratch_shapes=scratch,
        compiler_params=pltpu.CompilerParams(
            collective_id=0, has_side_effects=True, vmem_limit_bytes=60 * 1024 * 1024
        ),
        name="dino_head",
    )(hidden.T, w_last, student_protos, teacher_bneck, teacher_protos)
    proto_grad, weight_grad = pl.pallas_call(
        move,
        out_shape=shapes,
        in_specs=[spec] * 2,
        out_specs=(spec, spec),
        scratch_shapes=[vm((OWN, COLS), F32), vm((8, 8, DIM), F32), dma((4,))],
        name="move_results",
    )(*results)
    return proto_grad, weight_grad.reshape(64, DIM)


def solution(mesh):
    placed = (
        P("batch", "proto"),
        P("proto", None),
        P(None, "proto"),
        P("batch", None),
        P(None, "proto"),
    )
    return jax.shard_map(
        per_device,
        mesh=mesh,
        in_specs=placed,
        out_specs=(P("batch", "proto"), P("proto", None)),
        check_vma=False,
    )
```

```python
import functools

import jax
import jax.numpy as jnp
from jax import lax
from jax.experimental import pallas as pl
from jax.experimental.pallas import tpu as pltpu
from jax.sharding import PartitionSpec as P

PROTOS = 131072
CROPS = 6144
ITERS = 3
EPS = 1e-06
F32 = jnp.float32
BF16 = jnp.bfloat16
MESH = pl.DeviceIdType.MESH

ROWS = 384
COLS = 4096
DIM = 256
CHUNK = 512
WIDE = 1024
NCHUNK = COLS // CHUNK
HALF = COLS // 2
LANES = 128
NX, NZ, NY = 4, 8, 4
OWN = 16
SHARDS = 6


def ds(start, size):
    return pl.ds(pl.multiple_of(start, size), size)


def kernel(
    hidden_in, w_in, sp_in, tb_in, tp_in, out_pg, out_wg,
    hidden, w_last, sp, tb, tp, in_s, out_s,
    kexp, sexp, scols, cscale, trows, ub, wide, vrow, acc, sacc, part,
    xrecv, zsrc, zrecv, unit, rscale, srows, rowg, rxrecv, rzsrc, rzrecv, brows,
    nb, fsrc, fb, nbh, vh, xb1, zb1, xb, zb, xbs, zbs, kp, tpr, ubp, accp, lgs, colall, crecv, ysend, yrecv, zhsend, zhrecv, total,
    wsrc, wrecv, wfsrc, wfrecv, wfull,
    nb_s, nb_r, fb_s, fb_r, nh_s, nh_r, vh_s, vh_r, xb_s, xb_r, zb_s, zb_r,
    mi_s, mi_r, tx_s, tx_r, x_s, x_r, z_s, z_r, az_s, az_r, ax_s, ax_r,
    c_s, c_r, y_s, y_r, zh_s, zh_r, w_s, w_r, wf_s, wf_r, wg_s, wg_r,
):
    b = lax.axis_index("batch")
    p = lax.axis_index("proto")
    zh = b // 8
    k = b % 8
    y = k // 2
    c = b % 2
    z = p // NX
    x = p % NX

    def near(d):
        return {"batch": zh * 8 + (k + d) % 8, "proto": p}

    def far():
        return {"batch": (1 - zh) * 8 + k, "proto": p}

    def core():
        return {"batch": zh * 8 + y * 2 + (1 - c), "proto": p}

    def along_y(d):
        return {"batch": zh * 8 + ((y + d) % NY) * 2 + c, "proto": p}

    def along_x(d):
        return {"batch": b, "proto": z * NX + (x + d) % NX}

    def at_z(j):
        return {"batch": b, "proto": j * NX + x}

    gz = zh * NZ + z

    def ring(d):
        g = (gz + d) % 16
        return {"batch": (g // NZ) * 8 + k, "proto": (g % NZ) * NX + x}

    def mirror():
        return {"batch": (1 - zh) * 8 + k, "proto": (NZ - 1 - z) * NX + x}

    def remote(src, dst, ss, rs, dev):
        return pltpu.make_async_remote_copy(
            src_ref=src, dst_ref=dst, send_sem=ss, recv_sem=rs, device_id=dev, device_id_type=MESH
        )

    def await_bytes(ref, sem):
        pltpu.make_async_copy(ref, ref, sem).wait()

    def load(src, dst, i):
        return pltpu.make_async_copy(src, dst, in_s.at[i])

    def tp_load(i):
        cols = ds(i * WIDE, WIDE)
        return load(tp_in.at[:, cols], tp.at[:, cols], i)

    loads = [load(tb_in, tb, 4), load(hidden_in, hidden, 5), load(w_in, w_last, 6), load(sp_in, sp, 7)]
    loads[0].start()
    for i in range(COLS // WIDE):
        tp_load(i).start()
    for copy in loads[1:]:
        copy.start()

    barrier = pltpu.get_barrier_semaphore()

    def greet(dev):
        pl.semaphore_signal(barrier, inc=1, device_id=dev, device_id_type=MESH)

    for d in range(1, 8):
        greet(near(d))
    for d in range(1, NX):
        greet(along_x(d))
    for d in range(1, 16):
        greet(ring(d))

    loads[0].wait()
    t = tb[...].astype(F32)
    trows[...] = (t * lax.rsqrt(jnp.sum(t * t, axis=1, keepdims=True) + EPS)).astype(BF16)

    def store_sums(s, i, sums):
        nb[s, k, ds(i * 8, 8), :] = jnp.concatenate(sums, axis=0)

    def teacher_chunk(i, _):
        cols = ds(i * WIDE, WIDE)
        tp_load(i).wait()
        f = tp[:, cols].astype(F32)
        tc = (f * lax.rsqrt(jnp.sum(f * f, axis=0, keepdims=True) + EPS)).astype(BF16)
        e = jnp.exp(25.0 * jnp.dot(trows[...], tc, preferred_element_type=F32))
        tp[:, cols] = tc
        kexp[:, cols] = e
        sums = jnp.sum(e, axis=0, keepdims=True)
        store_sums(0, i, [sums[:, j * LANES : (j + 1) * LANES] for j in range(8)])
        return 0

    lax.fori_loop(0, COLS // WIDE, teacher_chunk, 0)
    pl.semaphore_wait(barrier, 25)

    def pack(s):
        for j in range(32):
            nb[s, k, j : j + 1, :] = wide[0:1, j * LANES : (j + 1) * LANES]

    def near_send(s):
        for d in range(1, 8):
            remote(nb.at[s, k], nb.at[s, k], nb_s.at[s], nb_r.at[s], near(d)).start()

    def near_wait(s):
        await_bytes(nb.at[s, pl.ds(0, 7)], nb_r.at[s])

    def far_send(s):
        fsrc[s] = jnp.sum(nb[s], axis=0)
        remote(fsrc.at[s], fb.at[s], fb_s.at[s], fb_r.at[s], far()).start()

    def far_wait(s):
        remote(fsrc.at[s], fb.at[s], fb_s.at[s], fb_r.at[s], far()).wait()
        await_bytes(nb.at[s, pl.ds(0, 7)], nb_s.at[s])
        return fsrc[s] + fb[s]

    def unpack(v):
        for j in range(32):
            vrow[0:1, j * LANES : (j + 1) * LANES] = v[j : j + 1, :]

    def lanes_of(ref, i):
        blk = ref[i * LANES : (i + 1) * LANES, :]
        return jnp.sum(blk.T, axis=0, keepdims=True)

    def rows_of(v):
        return jnp.broadcast_to(v, (LANES, LANES)).T

    def x_send(buf, s):
        for d in range(1, NX):
            remote(buf.at[x], buf.at[x], xb_s.at[s], xb_r.at[s], along_x(d)).start()

    def x_wait(buf, s):
        await_bytes(buf.at[pl.ds(0, 3)], xb_r.at[s])
        await_bytes(buf.at[pl.ds(0, 3)], xb_s.at[s])
        return jnp.sum(buf[...], axis=0)

    def z_send(buf, s, value):
        buf[gz] = value
        for d in range(1, 16):
            remote(buf.at[gz], buf.at[gz], zb_s.at[s], zb_r.at[s], ring(d)).start()

    def z_wait(buf, s):
        await_bytes(buf.at[pl.ds(0, 15)], zb_r.at[s])
        await_bytes(buf.at[pl.ds(0, 15)], zb_s.at[s])

    def row_pass(src, dst, col0, v0, chunks):
        def block(r, _):
            rows = ds(r * 64, 64)

            def step(i, a):
                q = src[rows, ds(col0 + i * CHUNK, CHUNK)] * vrow[0:1, ds(v0 + i * CHUNK, CHUNK)]
                for j in range(CHUNK // LANES):
                    a = a + q[:, j * LANES : (j + 1) * LANES]
                return a

            dst[rows, :] = lax.fori_loop(0, chunks, step, jnp.zeros((64, LANES), F32))
            return 0

        lax.fori_loop(0, ROWS // 64, block, 0)

    half0 = zh * HALF

    def half_rows(s):
        row_pass(kexp, acc, half0, half0, HALF // CHUNK)
        row_pass(kp, accp, 0, half0, HALF // CHUNK)
        for i in range(3):
            xb[s, x, zh, 0:1, i * LANES : (i + 1) * LANES] = lanes_of(acc, i)
            xb[s, x, 1 - zh, 0:1, i * LANES : (i + 1) * LANES] = lanes_of(accp, i)

    def half_cols(s):
        def step(i, _):
            sums = []
            for j in range(0, 8, 4):
                own = [ds(half0 + i * WIDE + (j + q) * LANES, LANES) for q in range(4)]
                other = [ds(i * WIDE + (j + q) * LANES, LANES) for q in range(4)]
                a = [jnp.zeros((8, LANES), F32)] * 4
                for r in range(0, ROWS, 8):
                    f = ub[r : r + 8, :]
                    g = ubp[r : r + 8, :]
                    for q in range(4):
                        a[q] = a[q] + kexp[r : r + 8, own[q]] * f + kp[r : r + 8, other[q]] * g
                sums += [jnp.sum(v, axis=0, keepdims=True) for v in a]
            nbh[s, k, ds(i * 8, 8), :] = jnp.concatenate(sums, axis=0)
            return 0

        lax.fori_loop(0, HALF // WIDE, step, 0)
        for d in range(1, 8):
            remote(nbh.at[s, k], nbh.at[s, k], nh_s.at[s], nh_r.at[s], near(d)).start()

    def half_scale(s):
        await_bytes(nbh.at[s, pl.ds(0, 7)], nh_r.at[s])
        await_bytes(nbh.at[s, pl.ds(0, 7)], nh_s.at[s])
        v = 1.0 / (PROTOS * jnp.sum(nbh[s], axis=0))
        for j in range(16):
            vrow[0:1, ds(half0 + j * LANES, LANES)] = v[j : j + 1, :]
        return v

    def rs_x_send(s, half, src, dst):
        for d in range(1, NX):
            rows = ds(half * 192 + ((x + d) % NX) * 48, 48)
            remote(
                src.at[rows], dst.at[half, d - 1], x_s.at[s, half], x_r.at[s, half], along_x(d)
            ).start()

    def rs_z_send(s, half, src, xr, zs, zr):
        await_bytes(xr.at[half], x_r.at[s, half])
        red = src[ds(half * 192 + x * 48, 48), :] + xr[half, 0] + xr[half, 1] + xr[half, 2]
        zs[half] = red.reshape(3, OWN, DIM)
        for jj in range(3):
            to = 2 * jj + half + 1

            @pl.when(z != to)
            def _():
                remote(zs.at[half, jj], zr.at[z], z_s.at[s], z_r.at[s], at_z(to)).start()

    owner = jnp.logical_and(z >= 1, z <= SHARDS)
    my_half = (z - 1) % 2
    my_rows = ds((z - 1) // 2 * OWN, OWN)

    def rs_z_wait(s, zs, zr):
        await_bytes(zr.at[pl.ds(0, 7)], z_r.at[s])
        zr[z] = zs[my_half, (z - 1) // 2]
        return jnp.sum(zr[...], axis=0)

    def rs_sent(s, xr, zr):
        for half in range(2):
            await_bytes(xr.at[half], x_s.at[s, half])

        @pl.when(owner)
        def _():
            await_bytes(zr.at[pl.ds(0, SHARDS - 1)], z_s.at[s])

        @pl.when(jnp.logical_not(owner))
        def _():
            await_bytes(zr.at[pl.ds(0, SHARDS)], z_s.at[s])

    def ag_z_send(s, full):
        ref = full.at[my_half, x, my_rows]
        for d in range(1, NZ):
            remote(ref, ref, az_s.at[s], az_r.at[s, z - 1], at_z((z + d) % NZ)).start()

    def ag_x_send(s, full):
        for j in range(SHARDS):
            @pl.when(z != j + 1)
            def _():
                await_bytes(full.at[j % 2, x, pl.ds(j // 2 * OWN, OWN)], az_r.at[s, j])

        for d in range(1, NX):
            remote(full.at[:, x], full.at[:, x], ax_s.at[s], ax_r.at[s], along_x(d)).start()

    def ag_wait(s, full):
        await_bytes(full.at[:, pl.ds(0, 3)], ax_r.at[s])
        await_bytes(full.at[:, pl.ds(0, 3)], ax_s.at[s])

        @pl.when(owner)
        def _():
            for d in range(1, NZ):
                await_bytes(full.at[0, 0, pl.ds(0, OWN)], az_s.at[s])

        return full[...].reshape(ROWS, DIM)

    near_send(0)
    loads[1].wait()
    loads[2].wait()
    part[...] = lax.dot_general(
        hidden[...], w_last[...], (((0,), (0,)), ((), ())), preferred_element_type=F32
    )
    rs_x_send(0, 0, part, xrecv)
    rs_x_send(0, 1, part, xrecv)
    loads[3].wait()

    def student_cols(i, _):
        cols = ds(i * CHUNK, CHUNK)
        f = sp[:, cols].astype(F32)
        sc = lax.rsqrt(jnp.sum(f * f, axis=0, keepdims=True) + EPS)
        cscale[0:1, cols] = sc
        scols[:, cols] = (f * sc).astype(BF16)
        return 0

    lax.fori_loop(0, NCHUNK, student_cols, 0)
    near_wait(0)
    far_send(0)

    teach = remote(trows.at[ds(x * 96, 96)], tpr.at[x], mi_s, mi_r, mirror())
    teach.start()
    unpack(1.0 / (PROTOS * far_wait(0)))
    row_pass(kexp, acc, 0, 0, NCHUNK)
    for i in range(3):
        xb1[x, 0:1, i * LANES : (i + 1) * LANES] = lanes_of(acc, i)
    x_send(xb1, 0)
    teach.wait()
    for d in range(1, NX):
        remote(tpr.at[x], tpr.at[x], tx_s, tx_r, along_x(d)).start()
    z_send(zb1, 0, x_wait(xb1, 0))
    rs_z_send(0, 0, part, xrecv, zsrc, zrecv)
    rs_z_send(0, 1, part, xrecv, zsrc, zrecv)
    await_bytes(tpr.at[pl.ds(0, 3)], tx_r)
    await_bytes(tpr.at[pl.ds(0, 3)], tx_s)

    def partner_chunk(i, _):
        cols = ds(half0 + i * WIDE, WIDE)
        rows = tpr[...].reshape(ROWS, DIM)
        kp[:, ds(i * WIDE, WIDE)] = jnp.exp(
            25.0 * jnp.dot(rows, tp[:, cols], preferred_element_type=F32)
        )
        return 0

    lax.fori_loop(0, HALF // WIDE, partner_chunk, 0)

    def crop_scale(total_):
        return 1.0 / (CROPS * total_)

    def set_u(dst, v):
        for i in range(3):
            dst[i * LANES : (i + 1) * LANES, :] = rows_of(v[:, i * LANES : (i + 1) * LANES])

    z_wait(zb1, 0)
    set_u(ub, crop_scale(jnp.sum(zb1[pl.ds(zh * NZ, NZ)], axis=0)))
    set_u(ubp, crop_scale(jnp.sum(zb1[pl.ds((1 - zh) * NZ, NZ)], axis=0)))

    half_cols(0)
    half_scale(0)
    half_rows(0)
    x_send(xb.at[0], 1)

    @pl.when(owner)
    def _():
        bott = rs_z_wait(0, zsrc, zrecv)
        sc = lax.rsqrt(jnp.sum(bott * bott, axis=1, keepdims=True) + EPS)
        u = bott * sc
        unit[...] = u
        rscale[...] = jnp.broadcast_to(sc, (OWN, DIM))
        srows[my_half, x, my_rows, :] = u.astype(BF16)
        ag_z_send(0, srows)

    z_send(zb.at[0], 1, x_wait(xb.at[0], 1))
    rs_sent(0, xrecv, zrecv)
    ag_x_send(0, srows)
    z_wait(zb.at[0], 1)

    def of_group(s, g):
        return crop_scale(jnp.sum(zb[s, :, g], axis=0))

    set_u(ub, of_group(0, zh))
    set_u(ubp, of_group(0, 1 - zh))

    half_cols(1)
    ag_wait(0, srows)
    sacc[...] = jnp.zeros_like(sacc)

    def student_chunk(i, _):
        cols = ds(i * CHUNK, CHUNK)
        rows = srows[...].reshape(ROWS, DIM)
        e = jnp.exp(10.0 * jnp.dot(rows, scols[:, cols], preferred_element_type=F32))
        sexp[:, cols] = e
        a = sacc[...]
        for j in range(CHUNK // LANES):
            a = a + e[:, j * LANES : (j + 1) * LANES]
        sacc[...] = a
        return 0

    lax.fori_loop(0, NCHUNK, student_chunk, 0)
    vh[zh] = half_scale(1)
    v_copy = remote(vh.at[zh], vh.at[zh], vh_s, vh_r, far())
    v_copy.start()
    half_rows(1)
    x_send(xb.at[1], 2)
    for i in range(3):
        xbs[x, 0:1, i * LANES : (i + 1) * LANES] = lanes_of(sacc, i)
    x_send(xbs, 3)
    zb[1, gz] = x_wait(xb.at[1], 2)
    for d in range(1, 16):
        part_ref = zb.at[1, gz, (gz + d) % 16 // NZ]
        remote(part_ref, part_ref, zb_s.at[2], zb_r.at[2], ring(d)).start()
    zbs[z] = x_wait(xbs, 3)
    for d in range(1, NZ):
        remote(zbs.at[z], zbs.at[z], zb_s.at[3], zb_r.at[3], at_z((z + d) % NZ)).start()
    rowg[...] = jnp.zeros_like(rowg)
    v_copy.wait()
    for h in range(2):
        for j in range(16):
            at = h * HALF + j * LANES
            vrow[0:1, at : at + LANES] = vh[h, j : j + 1, :]
    gain = PROTOS / 128 * 10.0
    await_bytes(zbs.at[pl.ds(0, 7)], zb_r.at[3])
    await_bytes(zbs.at[pl.ds(0, 7)], zb_s.at[3])
    set_u(sacc, gain / jnp.sum(zbs[...], axis=0))
    await_bytes(zb.at[1, pl.ds(0, 15), zh], zb_r.at[2])
    await_bytes(zb.at[1, pl.ds(0, 15), zh], zb_s.at[2])
    set_u(ub, (gain * CROPS) * of_group(1, zh))

    def c_copy(i):
        cols = ds(i * CHUNK, CHUNK)
        return remote(
            colall.at[:, 1 - c, :, cols], crecv.at[:, :, cols], c_s.at[i], c_r.at[i], core()
        )

    def y_copy(i, d):
        cols = ds(i * CHUNK, CHUNK)
        return remote(
            ysend.at[(y + d) % NY, :, :, cols], yrecv.at[d - 1, :, :, cols],
            y_s.at[i, d - 1], y_r.at[i, d - 1], along_y(d),
        )

    def zh_copy(i):
        cols = ds(i * CHUNK, CHUNK)
        return remote(zhsend.at[:, cols], zhrecv.at[:, cols], zh_s.at[i], zh_r.at[i], far())

    def y_send(i):
        cols = ds(i * CHUNK, CHUNK)
        c_copy(i).wait()
        for g in range(NY):
            for h in range(2):
                s = colall[h * NY + g, c, :, cols] + crecv[h * NY + g, :, cols]
                crecv[h * NY + g, :, cols] = s
                ysend[g, h, :, cols] = s.astype(BF16)
        for d in range(1, NY):
            y_copy(i, d).start()

    def zh_send(i, _):
        cols = ds(i * CHUNK, CHUNK)
        for d in range(1, NY):
            y_copy(i, d).wait()

        def over_y(h):
            s = crecv[h * NY + y, :, cols]
            for d in range(1, NY):
                s = s + yrecv[d - 1, h, :, cols].astype(F32)
            return s

        total[:, cols] = over_y(zh)
        zhsend[:, cols] = over_y(1 - zh).astype(BF16)
        zh_copy(i).start()
        return 0

    def grad_half(half):
        rows = slice(half * 192, half * 192 + 192)

        def step(i, _):
            cols = ds(i * WIDE, WIDE)
            pieces = []
            for j in range(WIDE // LANES):
                lane = ds(i * WIDE + j * LANES, LANES)
                targets = (kexp[rows, lane] * vrow[0:1, lane]) * ub[rows, :]
                pieces.append((sexp[rows, lane] * sacc[rows, :] - targets).astype(BF16))
            lg = jnp.concatenate(pieces, axis=1)
            lgs[rows, cols] = lg
            rowg[rows, :] += lax.dot_general(
                lg, scols[:, cols], (((1,), (1,)), ((), ())), preferred_element_type=F32
            )
            return 0

        lax.fori_loop(0, COLS // WIDE, step, 0)
        rs_x_send(1, half, rowg, rxrecv)

    def column_chunk(i, _):
        cols = ds(i * CHUNK, CHUNK)
        rows = srows[...].reshape(ROWS, DIM)
        colg = lax.dot_general(
            rows, lgs[:, cols], (((0,), (0,)), ((), ())), preferred_element_type=F32
        )
        colall[:, :, :, cols] = colg.reshape(8, 2, OWN, CHUNK)
        c_copy(i).start()
        un = sp[:, cols].astype(F32) * cscale[0:1, cols]
        wide[0:1, cols] = jnp.sum(un * colg, axis=0, keepdims=True)
        return 0

    def y_sends(i, _):
        y_send(i)
        return 0

    grad_half(0)
    grad_half(1)
    lax.fori_loop(0, NCHUNK, column_chunk, 0)
    pack(1)
    near_send(1)
    rs_z_send(1, 0, rowg, rxrecv, rzsrc, rzrecv)
    rs_z_send(1, 1, rowg, rxrecv, rzsrc, rzrecv)
    lax.fori_loop(0, NCHUNK, y_sends, 0)
    near_wait(1)
    far_send(1)

    @pl.when(owner)
    def _():
        g = rs_z_wait(1, rzsrc, rzrecv)
        u = unit[...]
        dot = jnp.sum(u * g, axis=1, keepdims=True)
        brows[my_half, x, my_rows, :] = (rscale[...] * (g - u * dot)).astype(BF16)
        ag_z_send(1, brows)

    ag_x_send(1, brows)
    lax.fori_loop(0, NCHUNK, zh_send, 0)
    unpack(far_wait(1))
    bg = ag_wait(1, brows)
    wg = jnp.dot(hidden[...], bg, preferred_element_type=F32)
    wsrc[...] = wg.reshape(8, 8, DIM)
    for d in range(1, 8):
        remote(wsrc.at[(k + d) % 8], wrecv.at[k], w_s, w_r, near(d)).start()

    def finish(i, _):
        cols = ds(i * CHUNK, CHUNK)
        zh_copy(i).wait()
        s = total[:, cols] + zhrecv[:, cols].astype(F32)
        sc = cscale[0:1, cols]
        un = sp[ds(b * OWN, OWN), cols].astype(F32) * sc
        total[:, cols] = sc * (s - un * vrow[0:1, cols])
        pltpu.make_async_copy(total.at[:, cols], out_pg.at[:, cols], out_s.at[i]).start()
        return 0

    await_bytes(wrecv.at[pl.ds(0, 7)], w_r)
    wrecv[k] = wsrc[k]
    wfsrc[...] = jnp.sum(wrecv[...], axis=0)
    wf = remote(wfsrc, wfrecv, wf_s, wf_r, far())
    wf.start()
    lax.fori_loop(0, NCHUNK, finish, 0)
    rs_sent(1, rxrecv, rzrecv)
    await_bytes(wsrc.at[pl.ds(0, 7)], w_s)
    wf.wait()
    wfull[k] = wfsrc[...] + wfrecv[...]
    for d in range(1, 8):
        remote(wfull.at[k], wfull.at[k], wg_s, wg_r, near(d)).start()
    await_bytes(wfull.at[pl.ds(0, 7)], wg_r)
    await_bytes(wfull.at[pl.ds(0, 7)], wg_s)
    last = pltpu.make_async_copy(wfull, out_wg, out_s.at[NCHUNK])
    last.start()

    def sent(i, _):
        cols = ds(i * CHUNK, CHUNK)
        pltpu.make_async_copy(total.at[:, cols], out_pg.at[:, cols], out_s.at[i]).wait()
        return 0

    lax.fori_loop(0, NCHUNK, sent, 0)
    last.wait()


def move(pg_in, wg_in, pg, wg, pg_buf, wg_buf, sem):
    stages = [(pg_in, pg_buf, pg), (wg_in, wg_buf, wg)]
    loads = [pltpu.make_async_copy(src, buf, sem.at[i]) for i, (src, buf, _) in enumerate(stages)]
    stores = [pltpu.make_async_copy(buf, dst, sem.at[2 + i]) for i, (_, buf, dst) in enumerate(stages)]
    for copy in loads:
        copy.start()
    for i in (1, 0):
        loads[i].wait()
        stores[i].start()
    for copy in stores:
        copy.wait()


def per_device(hidden, w_last, student_protos, teacher_bneck, teacher_protos):
    vm = pltpu.VMEM
    dma = pltpu.SemaphoreType.DMA
    scratch = [
        vm((64, ROWS), BF16), vm((64, DIM), BF16), vm((DIM, COLS), BF16), vm((ROWS, DIM), BF16),
        vm((DIM, COLS), BF16), dma((8,)), dma((NCHUNK + 1,)),
        vm((ROWS, COLS), F32), vm((ROWS, COLS), F32), vm((DIM, COLS), BF16), vm((8, COLS), F32),
        vm((ROWS, DIM), BF16), vm((ROWS, LANES), F32), vm((8, COLS), F32), vm((8, COLS), F32),
        vm((ROWS, LANES), F32), vm((ROWS, LANES), F32), vm((ROWS, DIM), F32),
        vm((2, 3, 48, DIM), F32), vm((2, 3, OWN, DIM), F32), vm((NZ, OWN, DIM), F32),
        vm((OWN, DIM), F32), vm((OWN, DIM), F32), vm((2, NX, 48, DIM), BF16), vm((ROWS, DIM), F32),
        vm((2, 3, 48, DIM), F32), vm((2, 3, OWN, DIM), F32), vm((NZ, OWN, DIM), F32),
        vm((2, NX, 48, DIM), BF16),
        vm((2, 8, 32, LANES), F32), vm((2, 32, LANES), F32), vm((2, 32, LANES), F32),
        vm((2, 8, 16, LANES), F32), vm((2, 16, LANES), F32),
        vm((NX, 1, ROWS), F32), vm((16, 1, ROWS), F32), vm((2, NX, 2, 1, ROWS), F32),
        vm((2, 16, 2, 1, ROWS), F32), vm((NX, 1, ROWS), F32), vm((NZ, 1, ROWS), F32),
        vm((ROWS, HALF), F32), vm((NX, 96, DIM), BF16), vm((ROWS, LANES), F32),
        vm((ROWS, LANES), F32),
        vm((ROWS, COLS), BF16), vm((8, 2, OWN, COLS), F32), vm((8, OWN, COLS), F32), vm((NY, 2, OWN, COLS), BF16),
        vm((3, 2, OWN, COLS), BF16), vm((OWN, COLS), BF16), vm((OWN, COLS), BF16),
        vm((OWN, COLS), F32),
        vm((8, 8, DIM), F32), vm((8, 8, DIM), F32), vm((8, DIM), F32), vm((8, DIM), F32),
        vm((8, 8, DIM), F32),
        dma((2,)), dma((2,)), dma((2,)), dma((2,)), dma((2,)), dma((2,)), dma, dma,
        dma((4,)), dma((4,)), dma((4,)), dma((4,)), dma, dma, dma, dma,
        dma((2, 2)), dma((2, 2)), dma((2,)), dma((2,)), dma((2,)), dma((2, SHARDS)), dma((2,)), dma((2,)),
        dma((NCHUNK,)), dma((NCHUNK,)), dma((NCHUNK, 3)), dma((NCHUNK, 3)),
        dma((NCHUNK,)), dma((NCHUNK,)), dma, dma, dma, dma, dma, dma,
    ]
    spec = pl.BlockSpec(memory_space=pl.ANY)
    shapes = (
        jax.ShapeDtypeStruct((OWN, COLS), F32),
        jax.ShapeDtypeStruct((8, 8, DIM), F32),
    )
    results = pl.pallas_call(
        kernel,
        out_shape=shapes,
        in_specs=[spec] * 5,
        out_specs=(spec, spec),
        scratch_shapes=scratch,
        compiler_params=pltpu.CompilerParams(
            collective_id=0, has_side_effects=True, vmem_limit_bytes=60 * 1024 * 1024
        ),
        name="dino_head",
    )(hidden.T, w_last, student_protos, teacher_bneck, teacher_protos)
    proto_grad, weight_grad = pl.pallas_call(
        move,
        out_shape=shapes,
        in_specs=[spec] * 2,
        out_specs=(spec, spec),
        scratch_shapes=[vm((OWN, COLS), F32), vm((8, 8, DIM), F32), dma((4,))],
        name="move_results",
    )(*results)
    return proto_grad, weight_grad.reshape(64, DIM)


def solution(mesh):
    placed = (
        P("batch", "proto"),
        P("proto", None),
        P(None, "proto"),
        P("batch", None),
        P(None, "proto"),
    )
    return jax.shard_map(
        per_device,
        mesh=mesh,
        in_specs=placed,
        out_specs=(P("batch", "proto"), P("proto", None)),
        check_vma=False,
    )
```

```python
import functools

import jax
import jax.numpy as jnp
from jax import lax
from jax.experimental import pallas as pl
from jax.experimental.pallas import tpu as pltpu
from jax.sharding import PartitionSpec as P

PROTOS = 131072
CROPS = 6144
ITERS = 3
EPS = 1e-06
F32 = jnp.float32
BF16 = jnp.bfloat16
MESH = pl.DeviceIdType.MESH

ROWS = 384
COLS = 4096
DIM = 256
CHUNK = 512
WIDE = 1024
NCHUNK = COLS // CHUNK
HALF = COLS // 2
LANES = 128
NX, NZ, NY = 4, 8, 4
OWN = 16
SHARDS = 6


def ds(start, size):
    return pl.ds(pl.multiple_of(start, size), size)


def kernel(
    hidden_in, w_in, sp_in, tb_in, tp_in, out_pg, out_wg,
    hidden, w_last, sp, tb, tp, in_s, out_s,
    kexp, sexp, scols, cscale, trows, ub, wide, vrow, acc, sacc, part,
    xrecv, zsrc, zrecv, unit, rscale, srows, rowg, rxrecv, rzsrc, rzrecv, brows,
    nb, fsrc, fb, nbh, vh, xb1, zb1, xb, zb, xbs, zbs, kp, tpr, ubp, accp, lgs, colall, crecv, ysend, yrecv, zhsend, zhrecv, total,
    wsrc, wrecv, wfsrc, wfrecv, wfull,
    nb_s, nb_r, fb_s, fb_r, nh_s, nh_r, vh_s, vh_r, xb_s, xb_r, zb_s, zb_r,
    mi_s, mi_r, tx_s, tx_r, x_s, x_r, z_s, z_r, az_s, az_r, ax_s, ax_r,
    c_s, c_r, y_s, y_r, zh_s, zh_r, w_s, w_r, wf_s, wf_r, wg_s, wg_r,
):
    b = lax.axis_index("batch")
    p = lax.axis_index("proto")
    zh = b // 8
    k = b % 8
    y = k // 2
    c = b % 2
    z = p // NX
    x = p % NX

    def near(d):
        return {"batch": zh * 8 + (k + d) % 8, "proto": p}

    def far():
        return {"batch": (1 - zh) * 8 + k, "proto": p}

    def core():
        return {"batch": zh * 8 + y * 2 + (1 - c), "proto": p}

    def along_y(d):
        return {"batch": zh * 8 + ((y + d) % NY) * 2 + c, "proto": p}

    def along_x(d):
        return {"batch": b, "proto": z * NX + (x + d) % NX}

    def at_z(j):
        return {"batch": b, "proto": j * NX + x}

    gz = zh * NZ + z

    def ring(d):
        g = (gz + d) % 16
        return {"batch": (g // NZ) * 8 + k, "proto": (g % NZ) * NX + x}

    def mirror():
        return {"batch": (1 - zh) * 8 + k, "proto": (NZ - 1 - z) * NX + x}

    def remote(src, dst, ss, rs, dev):
        return pltpu.make_async_remote_copy(
            src_ref=src, dst_ref=dst, send_sem=ss, recv_sem=rs, device_id=dev, device_id_type=MESH
        )

    def await_bytes(ref, sem):
        pltpu.make_async_copy(ref, ref, sem).wait()

    def load(src, dst, i):
        return pltpu.make_async_copy(src, dst, in_s.at[i])

    def tp_load(i):
        cols = ds(i * WIDE, WIDE)
        return load(tp_in.at[:, cols], tp.at[:, cols], i)

    loads = [load(tb_in, tb, 4), load(hidden_in, hidden, 5), load(w_in, w_last, 6), load(sp_in, sp, 7)]
    loads[0].start()
    for i in range(COLS // WIDE):
        tp_load(i).start()
    for copy in loads[1:]:
        copy.start()

    barrier = pltpu.get_barrier_semaphore()

    def greet(dev):
        pl.semaphore_signal(barrier, inc=1, device_id=dev, device_id_type=MESH)

    for d in range(1, 8):
        greet(near(d))
    for d in range(1, NX):
        greet(along_x(d))
    for d in range(1, 16):
        greet(ring(d))

    loads[0].wait()
    t = tb[...].astype(F32)
    trows[...] = (t * lax.rsqrt(jnp.sum(t * t, axis=1, keepdims=True) + EPS)).astype(BF16)

    def store_sums(s, i, sums):
        nb[s, k, ds(i * 8, 8), :] = jnp.concatenate(sums, axis=0)

    def teacher_chunk(i, _):
        cols = ds(i * WIDE, WIDE)
        tp_load(i).wait()
        f = tp[:, cols].astype(F32)
        tc = (f * lax.rsqrt(jnp.sum(f * f, axis=0, keepdims=True) + EPS)).astype(BF16)
        e = jnp.exp(25.0 * jnp.dot(trows[...], tc, preferred_element_type=F32))
        tp[:, cols] = tc
        kexp[:, cols] = e
        sums = jnp.sum(e, axis=0, keepdims=True)
        store_sums(0, i, [sums[:, j * LANES : (j + 1) * LANES] for j in range(8)])
        return 0

    lax.fori_loop(0, COLS // WIDE, teacher_chunk, 0)
    pl.semaphore_wait(barrier, 25)

    def pack(s):
        for j in range(32):
            nb[s, k, j : j + 1, :] = wide[0:1, j * LANES : (j + 1) * LANES]

    def near_send(s):
        for d in range(1, 8):
            remote(nb.at[s, k], nb.at[s, k], nb_s.at[s], nb_r.at[s], near(d)).start()

    def near_wait(s):
        await_bytes(nb.at[s, pl.ds(0, 7)], nb_r.at[s])

    def far_send(s):
        fsrc[s] = jnp.sum(nb[s], axis=0)
        remote(fsrc.at[s], fb.at[s], fb_s.at[s], fb_r.at[s], far()).start()

    def far_wait(s):
        remote(fsrc.at[s], fb.at[s], fb_s.at[s], fb_r.at[s], far()).wait()
        await_bytes(nb.at[s, pl.ds(0, 7)], nb_s.at[s])
        return fsrc[s] + fb[s]

    def unpack(v):
        for j in range(32):
            vrow[0:1, j * LANES : (j + 1) * LANES] = v[j : j + 1, :]

    def lanes_of(ref, i):
        blk = ref[i * LANES : (i + 1) * LANES, :]
        return jnp.sum(blk.T, axis=0, keepdims=True)

    def rows_of(v):
        return jnp.broadcast_to(v, (LANES, LANES)).T

    def x_send(buf, s):
        for d in range(1, NX):
            remote(buf.at[x], buf.at[x], xb_s.at[s], xb_r.at[s], along_x(d)).start()

    def x_wait(buf, s):
        await_bytes(buf.at[pl.ds(0, 3)], xb_r.at[s])
        await_bytes(buf.at[pl.ds(0, 3)], xb_s.at[s])
        return jnp.sum(buf[...], axis=0)

    def z_send(buf, s, value):
        buf[gz] = value
        for d in range(1, 16):
            remote(buf.at[gz], buf.at[gz], zb_s.at[s], zb_r.at[s], ring(d)).start()

    def z_wait(buf, s):
        await_bytes(buf.at[pl.ds(0, 15)], zb_r.at[s])
        await_bytes(buf.at[pl.ds(0, 15)], zb_s.at[s])

    def row_pass(src, dst, col0, v0, chunks):
        def block(r, _):
            rows = ds(r * 64, 64)

            a = jnp.zeros((64, LANES), F32)
            for j in range(chunks * CHUNK // LANES):
                at = j * LANES
                a = a + src[rows, ds(col0 + at, LANES)] * vrow[0:1, ds(v0 + at, LANES)]
            dst[rows, :] = a
            return 0

        lax.fori_loop(0, ROWS // 64, block, 0)

    half0 = zh * HALF

    def half_rows(s):
        row_pass(kexp, acc, half0, half0, HALF // CHUNK)
        row_pass(kp, accp, 0, half0, HALF // CHUNK)
        for i in range(3):
            xb[s, x, zh, 0:1, i * LANES : (i + 1) * LANES] = lanes_of(acc, i)
            xb[s, x, 1 - zh, 0:1, i * LANES : (i + 1) * LANES] = lanes_of(accp, i)

    def half_cols(s):
        def step(i, _):
            sums = []
            for j in range(0, 8, 4):
                own = [ds(half0 + i * WIDE + (j + q) * LANES, LANES) for q in range(4)]
                other = [ds(i * WIDE + (j + q) * LANES, LANES) for q in range(4)]
                a = [jnp.zeros((8, LANES), F32)] * 4
                for r in range(0, ROWS, 8):
                    f = ub[r : r + 8, :]
                    g = ubp[r : r + 8, :]
                    for q in range(4):
                        a[q] = a[q] + kexp[r : r + 8, own[q]] * f + kp[r : r + 8, other[q]] * g
                sums += [jnp.sum(v, axis=0, keepdims=True) for v in a]
            nbh[s, k, ds(i * 8, 8), :] = jnp.concatenate(sums, axis=0)
            return 0

        lax.fori_loop(0, HALF // WIDE, step, 0)
        for d in range(1, 8):
            remote(nbh.at[s, k], nbh.at[s, k], nh_s.at[s], nh_r.at[s], near(d)).start()

    def half_scale(s):
        await_bytes(nbh.at[s, pl.ds(0, 7)], nh_r.at[s])
        await_bytes(nbh.at[s, pl.ds(0, 7)], nh_s.at[s])
        v = 1.0 / (PROTOS * jnp.sum(nbh[s], axis=0))
        for j in range(16):
            vrow[0:1, ds(half0 + j * LANES, LANES)] = v[j : j + 1, :]
        return v

    def rs_x_send(s, half, src, dst):
        for d in range(1, NX):
            rows = ds(half * 192 + ((x + d) % NX) * 48, 48)
            remote(
                src.at[rows], dst.at[half, d - 1], x_s.at[s, half], x_r.at[s, half], along_x(d)
            ).start()

    def rs_z_send(s, half, src, xr, zs, zr):
        await_bytes(xr.at[half], x_r.at[s, half])
        red = src[ds(half * 192 + x * 48, 48), :] + xr[half, 0] + xr[half, 1] + xr[half, 2]
        zs[half] = red.reshape(3, OWN, DIM)
        for jj in range(3):
            to = 2 * jj + half + 1

            @pl.when(z != to)
            def _():
                remote(zs.at[half, jj], zr.at[z], z_s.at[s], z_r.at[s], at_z(to)).start()

    owner = jnp.logical_and(z >= 1, z <= SHARDS)
    my_half = (z - 1) % 2
    my_rows = ds((z - 1) // 2 * OWN, OWN)

    def rs_z_wait(s, zs, zr):
        await_bytes(zr.at[pl.ds(0, 7)], z_r.at[s])
        zr[z] = zs[my_half, (z - 1) // 2]
        return jnp.sum(zr[...], axis=0)

    def rs_sent(s, xr, zr):
        for half in range(2):
            await_bytes(xr.at[half], x_s.at[s, half])

        @pl.when(owner)
        def _():
            await_bytes(zr.at[pl.ds(0, SHARDS - 1)], z_s.at[s])

        @pl.when(jnp.logical_not(owner))
        def _():
            await_bytes(zr.at[pl.ds(0, SHARDS)], z_s.at[s])

    def ag_z_send(s, full):
        ref = full.at[my_half, x, my_rows]
        for d in range(1, NZ):
            remote(ref, ref, az_s.at[s], az_r.at[s, z - 1], at_z((z + d) % NZ)).start()

    def ag_x_send(s, full):
        for j in range(SHARDS):
            @pl.when(z != j + 1)
            def _():
                await_bytes(full.at[j % 2, x, pl.ds(j // 2 * OWN, OWN)], az_r.at[s, j])

        for d in range(1, NX):
            remote(full.at[:, x], full.at[:, x], ax_s.at[s], ax_r.at[s], along_x(d)).start()

    def ag_wait(s, full):
        await_bytes(full.at[:, pl.ds(0, 3)], ax_r.at[s])
        await_bytes(full.at[:, pl.ds(0, 3)], ax_s.at[s])

        @pl.when(owner)
        def _():
            for d in range(1, NZ):
                await_bytes(full.at[0, 0, pl.ds(0, OWN)], az_s.at[s])

        return full[...].reshape(ROWS, DIM)

    near_send(0)
    loads[1].wait()
    loads[2].wait()
    part[...] = lax.dot_general(
        hidden[...], w_last[...], (((0,), (0,)), ((), ())), preferred_element_type=F32
    )
    rs_x_send(0, 0, part, xrecv)
    rs_x_send(0, 1, part, xrecv)
    loads[3].wait()

    def student_cols(i, _):
        cols = ds(i * CHUNK, CHUNK)
        f = sp[:, cols].astype(F32)
        sc = lax.rsqrt(jnp.sum(f * f, axis=0, keepdims=True) + EPS)
        cscale[0:1, cols] = sc
        scols[:, cols] = (f * sc).astype(BF16)
        return 0

    lax.fori_loop(0, NCHUNK, student_cols, 0)
    near_wait(0)
    far_send(0)

    teach = remote(trows.at[ds(x * 96, 96)], tpr.at[x], mi_s, mi_r, mirror())
    teach.start()
    unpack(1.0 / (PROTOS * far_wait(0)))
    row_pass(kexp, acc, 0, 0, NCHUNK)
    for i in range(3):
        xb1[x, 0:1, i * LANES : (i + 1) * LANES] = lanes_of(acc, i)
    x_send(xb1, 0)
    teach.wait()
    for d in range(1, NX):
        remote(tpr.at[x], tpr.at[x], tx_s, tx_r, along_x(d)).start()
    z_send(zb1, 0, x_wait(xb1, 0))
    rs_z_send(0, 0, part, xrecv, zsrc, zrecv)
    rs_z_send(0, 1, part, xrecv, zsrc, zrecv)
    await_bytes(tpr.at[pl.ds(0, 3)], tx_r)
    await_bytes(tpr.at[pl.ds(0, 3)], tx_s)

    def partner_chunk(i, _):
        cols = ds(half0 + i * WIDE, WIDE)
        rows = tpr[...].reshape(ROWS, DIM)
        kp[:, ds(i * WIDE, WIDE)] = jnp.exp(
            25.0 * jnp.dot(rows, tp[:, cols], preferred_element_type=F32)
        )
        return 0

    lax.fori_loop(0, HALF // WIDE, partner_chunk, 0)

    def crop_scale(total_):
        return 1.0 / (CROPS * total_)

    def set_u(dst, v):
        for i in range(3):
            dst[i * LANES : (i + 1) * LANES, :] = rows_of(v[:, i * LANES : (i + 1) * LANES])

    z_wait(zb1, 0)
    set_u(ub, crop_scale(jnp.sum(zb1[pl.ds(zh * NZ, NZ)], axis=0)))
    set_u(ubp, crop_scale(jnp.sum(zb1[pl.ds((1 - zh) * NZ, NZ)], axis=0)))

    half_cols(0)
    half_scale(0)
    half_rows(0)
    x_send(xb.at[0], 1)

    @pl.when(owner)
    def _():
        bott = rs_z_wait(0, zsrc, zrecv)
        sc = lax.rsqrt(jnp.sum(bott * bott, axis=1, keepdims=True) + EPS)
        u = bott * sc
        unit[...] = u
        rscale[...] = jnp.broadcast_to(sc, (OWN, DIM))
        srows[my_half, x, my_rows, :] = u.astype(BF16)
        ag_z_send(0, srows)

    z_send(zb.at[0], 1, x_wait(xb.at[0], 1))
    rs_sent(0, xrecv, zrecv)
    ag_x_send(0, srows)
    z_wait(zb.at[0], 1)

    def of_group(s, g):
        return crop_scale(jnp.sum(zb[s, :, g], axis=0))

    set_u(ub, of_group(0, zh))
    set_u(ubp, of_group(0, 1 - zh))

    half_cols(1)
    ag_wait(0, srows)
    sacc[...] = jnp.zeros_like(sacc)

    def student_chunk(i, _):
        cols = ds(i * CHUNK, CHUNK)
        rows = srows[...].reshape(ROWS, DIM)
        e = jnp.exp(10.0 * jnp.dot(rows, scols[:, cols], preferred_element_type=F32))
        sexp[:, cols] = e
        a = sacc[...]
        for j in range(CHUNK // LANES):
            a = a + e[:, j * LANES : (j + 1) * LANES]
        sacc[...] = a
        return 0

    lax.fori_loop(0, NCHUNK, student_chunk, 0)
    vh[zh] = half_scale(1)
    v_copy = remote(vh.at[zh], vh.at[zh], vh_s, vh_r, far())
    v_copy.start()
    half_rows(1)
    x_send(xb.at[1], 2)
    for i in range(3):
        xbs[x, 0:1, i * LANES : (i + 1) * LANES] = lanes_of(sacc, i)
    x_send(xbs, 3)
    zb[1, gz] = x_wait(xb.at[1], 2)
    for d in range(1, 16):
        part_ref = zb.at[1, gz, (gz + d) % 16 // NZ]
        remote(part_ref, part_ref, zb_s.at[2], zb_r.at[2], ring(d)).start()
    zbs[z] = x_wait(xbs, 3)
    for d in range(1, NZ):
        remote(zbs.at[z], zbs.at[z], zb_s.at[3], zb_r.at[3], at_z((z + d) % NZ)).start()
    rowg[...] = jnp.zeros_like(rowg)
    v_copy.wait()
    for h in range(2):
        for j in range(16):
            at = h * HALF + j * LANES
            vrow[0:1, at : at + LANES] = vh[h, j : j + 1, :]
    gain = PROTOS / 128 * 10.0
    await_bytes(zbs.at[pl.ds(0, 7)], zb_r.at[3])
    await_bytes(zbs.at[pl.ds(0, 7)], zb_s.at[3])
    set_u(sacc, gain / jnp.sum(zbs[...], axis=0))
    await_bytes(zb.at[1, pl.ds(0, 15), zh], zb_r.at[2])
    await_bytes(zb.at[1, pl.ds(0, 15), zh], zb_s.at[2])
    set_u(ub, (gain * CROPS) * of_group(1, zh))

    def c_copy(i):
        cols = ds(i * CHUNK, CHUNK)
        return remote(
            colall.at[:, 1 - c, :, cols], crecv.at[:, :, cols], c_s.at[i], c_r.at[i], core()
        )

    def y_copy(i, d):
        cols = ds(i * CHUNK, CHUNK)
        return remote(
            ysend.at[(y + d) % NY, :, :, cols], yrecv.at[d - 1, :, :, cols],
            y_s.at[i, d - 1], y_r.at[i, d - 1], along_y(d),
        )

    def zh_copy(i):
        cols = ds(i * CHUNK, CHUNK)
        return remote(zhsend.at[:, cols], zhrecv.at[:, cols], zh_s.at[i], zh_r.at[i], far())

    def y_send(i):
        cols = ds(i * CHUNK, CHUNK)
        c_copy(i).wait()
        for g in range(NY):
            for h in range(2):
                s = colall[h * NY + g, c, :, cols] + crecv[h * NY + g, :, cols]
                crecv[h * NY + g, :, cols] = s
                ysend[g, h, :, cols] = s.astype(BF16)
        for d in range(1, NY):
            y_copy(i, d).start()

    def zh_send(i, _):
        cols = ds(i * CHUNK, CHUNK)
        for d in range(1, NY):
            y_copy(i, d).wait()

        def over_y(h):
            s = crecv[h * NY + y, :, cols]
            for d in range(1, NY):
                s = s + yrecv[d - 1, h, :, cols].astype(F32)
            return s

        total[:, cols] = over_y(zh)
        zhsend[:, cols] = over_y(1 - zh).astype(BF16)
        zh_copy(i).start()
        return 0

    def grad_half(half):
        rows = slice(half * 192, half * 192 + 192)

        def step(i, _):
            cols = ds(i * WIDE, WIDE)
            pieces = []
            for j in range(WIDE // LANES):
                lane = ds(i * WIDE + j * LANES, LANES)
                targets = (kexp[rows, lane] * vrow[0:1, lane]) * ub[rows, :]
                pieces.append((sexp[rows, lane] * sacc[rows, :] - targets).astype(BF16))
            lg = jnp.concatenate(pieces, axis=1)
            lgs[rows, cols] = lg
            rowg[rows, :] += lax.dot_general(
                lg, scols[:, cols], (((1,), (1,)), ((), ())), preferred_element_type=F32
            )
            return 0

        lax.fori_loop(0, COLS // WIDE, step, 0)
        rs_x_send(1, half, rowg, rxrecv)

    def column_chunk(i, _):
        cols = ds(i * CHUNK, CHUNK)
        rows = srows[...].reshape(ROWS, DIM)
        colg = lax.dot_general(
            rows, lgs[:, cols], (((0,), (0,)), ((), ())), preferred_element_type=F32
        )
        colall[:, :, :, cols] = colg.reshape(8, 2, OWN, CHUNK)
        c_copy(i).start()
        un = sp[:, cols].astype(F32) * cscale[0:1, cols]
        wide[0:1, cols] = jnp.sum(un * colg, axis=0, keepdims=True)
        return 0

    def y_sends(i, _):
        y_send(i)
        return 0

    grad_half(0)
    grad_half(1)
    lax.fori_loop(0, NCHUNK, column_chunk, 0)
    pack(1)
    near_send(1)
    rs_z_send(1, 0, rowg, rxrecv, rzsrc, rzrecv)
    rs_z_send(1, 1, rowg, rxrecv, rzsrc, rzrecv)
    lax.fori_loop(0, NCHUNK, y_sends, 0)
    near_wait(1)
    far_send(1)

    @pl.when(owner)
    def _():
        g = rs_z_wait(1, rzsrc, rzrecv)
        u = unit[...]
        dot = jnp.sum(u * g, axis=1, keepdims=True)
        brows[my_half, x, my_rows, :] = (rscale[...] * (g - u * dot)).astype(BF16)
        ag_z_send(1, brows)

    ag_x_send(1, brows)
    lax.fori_loop(0, NCHUNK, zh_send, 0)
    unpack(far_wait(1))
    bg = ag_wait(1, brows)
    wg = jnp.dot(hidden[...], bg, preferred_element_type=F32)
    wsrc[...] = wg.reshape(8, 8, DIM)
    for d in range(1, 8):
        remote(wsrc.at[(k + d) % 8], wrecv.at[k], w_s, w_r, near(d)).start()

    def finish(i, _):
        cols = ds(i * CHUNK, CHUNK)
        zh_copy(i).wait()
        s = total[:, cols] + zhrecv[:, cols].astype(F32)
        sc = cscale[0:1, cols]
        un = sp[ds(b * OWN, OWN), cols].astype(F32) * sc
        total[:, cols] = sc * (s - un * vrow[0:1, cols])
        pltpu.make_async_copy(total.at[:, cols], out_pg.at[:, cols], out_s.at[i]).start()
        return 0

    await_bytes(wrecv.at[pl.ds(0, 7)], w_r)
    wrecv[k] = wsrc[k]
    wfsrc[...] = jnp.sum(wrecv[...], axis=0)
    wf = remote(wfsrc, wfrecv, wf_s, wf_r, far())
    wf.start()
    lax.fori_loop(0, NCHUNK, finish, 0)
    rs_sent(1, rxrecv, rzrecv)
    await_bytes(wsrc.at[pl.ds(0, 7)], w_s)
    wf.wait()
    wfull[k] = wfsrc[...] + wfrecv[...]
    for d in range(1, 8):
        remote(wfull.at[k], wfull.at[k], wg_s, wg_r, near(d)).start()
    await_bytes(wfull.at[pl.ds(0, 7)], wg_r)
    await_bytes(wfull.at[pl.ds(0, 7)], wg_s)
    last = pltpu.make_async_copy(wfull, out_wg, out_s.at[NCHUNK])
    last.start()

    def sent(i, _):
        cols = ds(i * CHUNK, CHUNK)
        pltpu.make_async_copy(total.at[:, cols], out_pg.at[:, cols], out_s.at[i]).wait()
        return 0

    lax.fori_loop(0, NCHUNK, sent, 0)
    last.wait()


def move(pg_in, wg_in, pg, wg, pg_buf, wg_buf, sem):
    stages = [(pg_in, pg_buf, pg), (wg_in, wg_buf, wg)]
    loads = [pltpu.make_async_copy(src, buf, sem.at[i]) for i, (src, buf, _) in enumerate(stages)]
    stores = [pltpu.make_async_copy(buf, dst, sem.at[2 + i]) for i, (_, buf, dst) in enumerate(stages)]
    for copy in loads:
        copy.start()
    for i in (1, 0):
        loads[i].wait()
        stores[i].start()
    for copy in stores:
        copy.wait()


def per_device(hidden, w_last, student_protos, teacher_bneck, teacher_protos):
    vm = pltpu.VMEM
    dma = pltpu.SemaphoreType.DMA
    scratch = [
        vm((64, ROWS), BF16), vm((64, DIM), BF16), vm((DIM, COLS), BF16), vm((ROWS, DIM), BF16),
        vm((DIM, COLS), BF16), dma((8,)), dma((NCHUNK + 1,)),
        vm((ROWS, COLS), F32), vm((ROWS, COLS), F32), vm((DIM, COLS), BF16), vm((8, COLS), F32),
        vm((ROWS, DIM), BF16), vm((ROWS, LANES), F32), vm((8, COLS), F32), vm((8, COLS), F32),
        vm((ROWS, LANES), F32), vm((ROWS, LANES), F32), vm((ROWS, DIM), F32),
        vm((2, 3, 48, DIM), F32), vm((2, 3, OWN, DIM), F32), vm((NZ, OWN, DIM), F32),
        vm((OWN, DIM), F32), vm((OWN, DIM), F32), vm((2, NX, 48, DIM), BF16), vm((ROWS, DIM), F32),
        vm((2, 3, 48, DIM), F32), vm((2, 3, OWN, DIM), F32), vm((NZ, OWN, DIM), F32),
        vm((2, NX, 48, DIM), BF16),
        vm((2, 8, 32, LANES), F32), vm((2, 32, LANES), F32), vm((2, 32, LANES), F32),
        vm((2, 8, 16, LANES), F32), vm((2, 16, LANES), F32),
        vm((NX, 1, ROWS), F32), vm((16, 1, ROWS), F32), vm((2, NX, 2, 1, ROWS), F32),
        vm((2, 16, 2, 1, ROWS), F32), vm((NX, 1, ROWS), F32), vm((NZ, 1, ROWS), F32),
        vm((ROWS, HALF), F32), vm((NX, 96, DIM), BF16), vm((ROWS, LANES), F32),
        vm((ROWS, LANES), F32),
        vm((ROWS, COLS), BF16), vm((8, 2, OWN, COLS), F32), vm((8, OWN, COLS), F32), vm((NY, 2, OWN, COLS), BF16),
        vm((3, 2, OWN, COLS), BF16), vm((OWN, COLS), BF16), vm((OWN, COLS), BF16),
        vm((OWN, COLS), F32),
        vm((8, 8, DIM), F32), vm((8, 8, DIM), F32), vm((8, DIM), F32), vm((8, DIM), F32),
        vm((8, 8, DIM), F32),
        dma((2,)), dma((2,)), dma((2,)), dma((2,)), dma((2,)), dma((2,)), dma, dma,
        dma((4,)), dma((4,)), dma((4,)), dma((4,)), dma, dma, dma, dma,
        dma((2, 2)), dma((2, 2)), dma((2,)), dma((2,)), dma((2,)), dma((2, SHARDS)), dma((2,)), dma((2,)),
        dma((NCHUNK,)), dma((NCHUNK,)), dma((NCHUNK, 3)), dma((NCHUNK, 3)),
        dma((NCHUNK,)), dma((NCHUNK,)), dma, dma, dma, dma, dma, dma,
    ]
    spec = pl.BlockSpec(memory_space=pl.ANY)
    shapes = (
        jax.ShapeDtypeStruct((OWN, COLS), F32),
        jax.ShapeDtypeStruct((8, 8, DIM), F32),
    )
    results = pl.pallas_call(
        kernel,
        out_shape=shapes,
        in_specs=[spec] * 5,
        out_specs=(spec, spec),
        scratch_shapes=scratch,
        compiler_params=pltpu.CompilerParams(
            collective_id=0, has_side_effects=True, vmem_limit_bytes=60 * 1024 * 1024
        ),
        name="dino_head",
    )(hidden.T, w_last, student_protos, teacher_bneck, teacher_protos)
    proto_grad, weight_grad = pl.pallas_call(
        move,
        out_shape=shapes,
        in_specs=[spec] * 2,
        out_specs=(spec, spec),
        scratch_shapes=[vm((OWN, COLS), F32), vm((8, 8, DIM), F32), dma((4,))],
        name="move_results",
    )(*results)
    return proto_grad, weight_grad.reshape(64, DIM)


def solution(mesh):
    placed = (
        P("batch", "proto"),
        P("proto", None),
        P(None, "proto"),
        P("batch", None),
        P(None, "proto"),
    )
    return jax.shard_map(
        per_device,
        mesh=mesh,
        in_specs=placed,
        out_specs=(P("batch", "proto"), P("proto", None)),
        check_vma=False,
    )
```
